32 devices in a mesh: row: 4 (over y, x), col: 8 (over z, core).
Axes of the slice: x: 2, y: 2, z: 4, core: 2. Of those that a mesh axis runs over, the one named last changes fastest.
Arguments:
- matrix: float32 [4096, 4096], P('row', 'col'), may hold values from -8 to 48
- pivots: int32 [2, 128], replicated, may hold values from 256 to 4095, as said below
- lower_inverse: float32 [2, 128, 128], replicated, may hold values from -1 to 1, as said below
Outputs:
- factored: float32 [4096, 4096], P('row', 'col')
The draws below stay inside these ranges and needn't reach their ends.
Inputs may be any that keep to these rules, and one draw needn't show every extreme that they name: pivots[k, j] is the global row that panel k exchanges with global row k * 128 + j; all 256 entries are distinct. Each lower_inverse[k] is unit lower triangular.
All inputs are finite; a program needn't handle non-finite values.
Results may differ from the reference program's by a relative error of at most 0.0001.
Values sent between devices are 32-bit elements; how exact they have to be, the bound alone decides.
A program may use at most 64 MiB of HBM per device.

```python
import jax
import jax.numpy as jnp
from jax import lax

NB = 128
CB = 4
PANELS = 2
GRID_ROWS = 4
GRID_COLS = 8
RB = 8
ORDER = 4096


def pivot_table(key):
    inner_rows = jax.random.permutation(jax.random.fold_in(key, 11), ORDER - 2 * NB - 2).astype(jnp.int32) + 2 * NB + 1
    chosen = jnp.concatenate([inner_rows[:2 * NB - 2], jnp.array([2 * NB, ORDER - 1], dtype=jnp.int32)])
    shuffle = jax.random.permutation(jax.random.fold_in(key, 12), 2 * NB)
    return chosen[shuffle].reshape(PANELS, NB).astype(jnp.int32)


def draw_pivots(key, part):
    return pivot_table(key)


def draw_matrix(key, part):
    pivot_rows = pivot_table(key)
    grid_rows = ORDER // (RB * NB)
    grid_cols = ORDER // (CB * NB)
    target = jnp.full((ORDER,), -1, dtype=jnp.int32).at[pivot_rows.reshape(-1)].set(jnp.arange(PANELS * NB, dtype=jnp.int32))
    spots = jnp.arange(ORDER, dtype=jnp.int32)
    global_row = (spots % (RB * NB) // NB * grid_rows + spots // (RB * NB)) * NB + spots % NB
    global_col = (spots % (CB * NB) // NB * grid_cols + spots // (CB * NB)) * NB + spots % NB
    row_target = target[global_row]
    boost = jnp.where(global_col[None, :] == row_target[:, None], 40.0, 0.0).astype(jnp.float32)
    noise_key = jax.random.fold_in(key, 21)
    noise = jnp.clip(jax.random.normal(noise_key, (ORDER, ORDER), jnp.float32), -4.0, 4.0)
    return (noise + boost).astype(jnp.float32)


def draw_lower_inverse(key, part):
    values = jnp.clip(jax.random.normal(key, (PANELS, NB, NB), jnp.float32), -4.0, 4.0) * (0.5 * NB ** (-0.5))
    tri_rows = jnp.arange(NB)[:, None]
    tri_cols = jnp.arange(NB)[None, :]
    return jnp.where(tri_rows > tri_cols, values, jnp.where(tri_rows == tri_cols, 1.0, 0.0)).astype(jnp.float32)


def setup_inputs(seed: int = 0) -> dict:
    seeds = jax.random.split(jax.random.key(seed), 4)
    return {
        "matrix": draw_matrix(jax.random.fold_in(seeds[3], 71), 0),
        "pivots": draw_pivots(jax.random.fold_in(seeds[3], 71), 0),
        "lower_inverse": draw_lower_inverse(jax.random.fold_in(seeds[3], 71), 0),
    }


def reference(matrix, pivots, lower_inverse):
    global_mat = matrix.reshape(GRID_ROWS, RB, NB, GRID_COLS, CB, NB).transpose(1, 0, 2, 4, 3, 5).reshape(ORDER, ORDER)
    for panel_num in range(PANELS):
        first_row = panel_num * NB
        past_row = first_row + NB
        pivot_rows = pivots[panel_num]
        top_rows = global_mat[first_row:past_row]
        taken_rows = global_mat[pivot_rows]
        global_mat = global_mat.at[pivot_rows].set(top_rows).at[first_row:past_row].set(taken_rows)
        product = jnp.dot(lower_inverse[panel_num].astype(jnp.float32), global_mat[first_row:past_row, first_row:].astype(jnp.float32), precision=lax.Precision.HIGHEST, preferred_element_type=jnp.float32)
        diag_part = jnp.triu(product[:, :NB])
        global_mat = global_mat.at[first_row:past_row, first_row:past_row].set(diag_part)
        global_mat = global_mat.at[first_row:past_row, past_row:].set(product[:, NB:])
        panel_cols = global_mat[past_row:, first_row:past_row]
        lower_block = jax.scipy.linalg.solve_triangular(diag_part, panel_cols.T, trans=1, lower=False).T
        global_mat = global_mat.at[past_row:, first_row:past_row].set(lower_block)
        change = jnp.dot(lower_block.astype(jnp.float32), product[:, NB:].astype(jnp.float32), precision=lax.Precision.HIGHEST, preferred_element_type=jnp.float32)
        global_mat = global_mat.at[past_row:, past_row:].set(global_mat[past_row:, past_row:] - change)
    return global_mat.reshape(RB, GRID_ROWS, NB, CB, GRID_COLS, NB).transpose(1, 0, 2, 4, 3, 5).reshape(ORDER, ORDER)
```

```python
import functools

import jax
import jax.numpy as jnp
from jax import lax
from jax.experimental import pallas as pl
from jax.experimental.pallas import tpu as pltpu
from jax.sharding import PartitionSpec as P

MESH = pl.DeviceIdType.MESH
F32 = jnp.float32
BF16 = jnp.bfloat16
CHUNKS = 16
EARLY = 3
MIDDLE = 9
ANY_EARLY = 3
TILES = 4


def mm(left, right):
    return jnp.dot(left, right, preferred_element_type=F32)


def exact(left, right):
    return jnp.dot(left, right, precision=lax.Precision.HIGHEST, preferred_element_type=F32)


def halves(value):
    high = value.astype(BF16)
    return high, (value - high.astype(F32)).astype(BF16)


def thirds(value):
    high = value.astype(BF16)
    rest = value - high.astype(F32)
    middle = rest.astype(BF16)
    return high, middle, (rest - middle.astype(F32)).astype(BF16)


def select(chosen, value):
    high, middle, low = thirds(value)
    return mm(chosen, high) + (mm(chosen, middle) + mm(chosen, low))


def dot3(left, right):
    left_high, left_low = left
    right_high, right_low = right
    return mm(left_high, right_high) + (mm(left_low, right_high) + mm(left_high, right_low))


def upper_inverse(upper, rows, cols):
    on_diag = rows == cols
    eye = jnp.where(on_diag, 1.0, 0.0)
    kept = jnp.where(on_diag, upper, 0.0)
    scaled = upper / jnp.sum(kept, axis=1, keepdims=True)
    power = jnp.where(rows < cols, -scaled, 0.0)
    result = eye + power
    reach = 2
    while reach < upper.shape[0]:
        power = exact(power, power)
        result = result + exact(result, power)
        reach = reach * 2
    return result / jnp.sum(kept, axis=0, keepdims=True)


def room(R, nb):
    return (nb // R + 31) // 16 * 16


def kernel(R, C, nb, a_hbm, piv_ref, linv_ref, asw,
           sel, sel_t, place, split, tcomp, pall, dall, tops, tpan, dh, pan, res, lt_hi, lt_lo,
           me_hi, me_lo, u_hi, u_lo, u_f, hit,
           load_sem, tq_s, tq_r, da_s, da_r, to_s, to_r,
           ag_s, ag_r, ch_s, ch_r, sb_s, sb_r):
    height, width = asw.shape
    two = 2 * nb
    cap = room(R, nb)
    W = 2 * cap
    ck = height // CHUNKS
    NJ = width // nb
    r = lax.axis_index("row")
    c = lax.axis_index("col")
    s = lax.rem(c, 2)
    sibling = {"col": c + 1 - 2 * s}
    top_half = jnp.minimum(r, 1)
    odd = lax.rem(r, 2)
    relay = R == 4

    def flip(bit):
        if bit == 1:
            return r + 1 - 2 * odd
        if bit == 2:
            return lax.rem(r + 2, 4)
        return 3 - r

    def cols(j):
        return pl.ds(j * nb, nb)

    def load(j):
        return pltpu.make_async_copy(a_hbm.at[:, cols(j)], asw.at[:, cols(j)], load_sem.at[j])

    for j in range(NJ):
        load(j).start()

    has_after = c + 2 < C
    has_before = c >= 2
    at_root = c < 2
    is_top = r < 2

    barrier = pltpu.get_barrier_semaphore()
    for off in range(1, R):
        pl.semaphore_signal(barrier, inc=1, device_id={"row": lax.rem(r + off, R)}, device_id_type=MESH)

    @pl.when(has_after)
    def _():
        pl.semaphore_signal(barrier, inc=1, device_id={"col": jnp.minimum(c + 2, C - 1)}, device_id_type=MESH)

    @pl.when(has_before)
    def _():
        pl.semaphore_signal(barrier, inc=1, device_id={"col": jnp.maximum(c - 2, 0)}, device_id_type=MESH)

    pl.semaphore_signal(barrier, inc=1, device_id=sibling, device_id_type=MESH)

    shift = nb.bit_length() - 1
    rshift = R.bit_length() - 1
    lane = lax.broadcasted_iota(jnp.int32, (nb, nb), 1)
    sub = lax.broadcasted_iota(jnp.int32, (nb, nb), 0)
    lane_f = lane.astype(F32)
    sub_f = sub.astype(F32)
    before = jnp.where(sub < lane, 1.0, 0.0).astype(BF16)
    owners, slots, talls = [], [], []
    for k in range(2):
        p = piv_ref[k:k + 1, :]
        block = jnp.right_shift(p, shift)
        owner = jnp.bitwise_and(block, R - 1)
        local = jnp.left_shift(jnp.right_shift(block, rshift), shift) + jnp.bitwise_and(p, nb - 1)
        hot = jnp.where(jnp.broadcast_to(owner, (16, nb)) == sub[0:16], 1.0, 0.0)
        rank = mm(hot.astype(BF16), before)
        slot = jnp.sum(hot * rank, axis=0, keepdims=True)
        mine = jnp.where(owner == r, slot, -1.0)
        match = jnp.broadcast_to(mine, (cap, nb)) == sub_f[0:cap]
        value = jnp.broadcast_to(local.astype(F32) + 1.0, (cap, nb))
        spot = jnp.sum(jnp.where(match, value, 0.0), axis=1, keepdims=True) - 1.0
        owners.append(owner)
        slots.append(slot)
        talls.append(jnp.broadcast_to(spot, (cap, nb)))
    if W < nb:
        talls.append(jnp.full((nb - W, nb), -1.0, F32))
    tall = jnp.concatenate(talls, axis=0)
    for t in range(height // nb):
        spots = slice(t * nb, (t + 1) * nb)
        sel_t[:, spots] = jnp.where(tall[0:W] == lane_f[0:W] + float(t * nb), 1.0, 0.0).astype(BF16)

    pl.semaphore_wait(barrier, R + jnp.minimum(c // 2, 1) + jnp.minimum((C - 1 - c) // 2, 1))

    def remote(src, dst, send, recv, where):
        return pltpu.make_async_remote_copy(
            src_ref=src, dst_ref=dst, send_sem=send, recv_sem=recv, device_id=where, device_id_type=MESH)

    def rows(index, count):
        return pl.ds(pl.multiple_of(index * count, count), count)

    def peer(off):
        return lax.rem(r + off, R)

    def origin(off):
        return lax.rem(r - off + R, R)

    def da_copy(off):
        part = dall.at[s, rows(r, W)]
        return remote(part, part, da_s.at[off - 1], da_r.at[off - 1], {"row": peer(off)})

    def da_in(off):
        part = dall.at[s, rows(origin(off), W)]
        return remote(part, part, da_s.at[off - 1], da_r.at[off - 1], {"row": peer(off)})

    def tq_copy(off):
        return remote(tcomp.at[0, rows(peer(off), cap)], tpan.at[s, rows(top_half, cap)],
                      tq_s.at[off - 1], tq_r.at[top_half], {"row": peer(off)})

    def tz_copy(off):
        return remote(tcomp.at[0, rows(peer(off), cap)], tops.at[0, rows(top_half, cap)],
                      tq_s.at[off - 1], tq_r.at[top_half], {"row": peer(off)})

    def to_copy(off):
        return remote(tcomp.at[pl.ds(1, NJ - 1), rows(peer(off), cap)],
                      tops.at[pl.ds(1, NJ - 1), rows(top_half, cap)],
                      to_s.at[off - 1], to_r.at[top_half], {"row": peer(off)})

    def tq_in(half):
        part = tpan.at[s, pl.ds(half * cap, cap)]
        return remote(part, part, tq_s.at[0], tq_r.at[half], {"row": peer(1)})

    def tz_in(half):
        part = tops.at[0, pl.ds(half * cap, cap)]
        return remote(part, part, tq_s.at[0], tq_r.at[half], {"row": peer(1)})

    def to_in(half):
        part = tops.at[pl.ds(1, NJ - 1), pl.ds(half * cap, cap)]
        return remote(part, part, to_s.at[0], to_r.at[half], {"row": peer(1)})

    def from_tops(copy):
        for half in range(2):
            @pl.when(r != half)
            def _():
                copy(half).wait_recv()

    def ag_copy(j, i):
        at = j * (R - 1) + i
        if not relay:
            part = pall.at[j, rows(r, W)]
            return remote(part, part, ag_s.at[at], ag_r.at[at], {"row": peer(i + 1)})
        if i < 2:
            part = pall.at[j, rows(r, W)]
            return remote(part, part, ag_s.at[at], ag_r.at[at], {"row": flip(i + 1)})
        bit = 1 + j % 2
        part = pall.at[j, rows(flip(3 - bit), W)]
        return remote(part, part, ag_s.at[at], ag_r.at[at], {"row": flip(bit)})

    def ag_in(j, i):
        at = j * (R - 1) + i
        src = flip(i + 1) if relay else origin(i + 1)
        part = pall.at[j, rows(src, W)]
        return remote(part, part, ag_s.at[at], ag_r.at[at], {"row": peer(1)})

    def ag_start(j):
        for i in range(2 if relay else R - 1):
            ag_copy(j, i).start()

    def ag_relay_from(j):
        return 1 - j % 2

    def past_root(j, go):
        if j == 0:
            pl.when(has_before)(go)
        else:
            go()

    def ag_pass(j):
        if relay:
            def go():
                ag_in(j, ag_relay_from(j)).wait_recv()
                ag_copy(j, 2).start()
            past_root(j, go)

    def ag_finish(j):
        def go():
            for i in range(R - 1):
                if not (relay and i == ag_relay_from(j)):
                    ag_in(j, i).wait_recv()
        past_root(j, go)

    TQ, DQ = CHUNKS, CHUNKS + 1

    def piece(k):
        if k < CHUNKS:
            return pan.at[s, pl.ds(k * ck, ck)]
        if k == TQ:
            return tpan.at[s, pl.ds(0, W)]
        return dall.at[s, rows(r, W)]

    after = {"col": jnp.minimum(c + 2, C - 2 + s)}

    def chain_copy(k):
        return remote(piece(k), piece(k), ch_s.at[k], ch_r.at[k], after)

    def root_copy(k):
        return remote(a_hbm.at[pl.ds(k * ck, ck), cols(0)], piece(k), ch_s.at[k], ch_r.at[k], after)

    def spread(k, side):
        if k < CHUNKS:
            return pan.at[side, pl.ds(k * ck, ck)]
        return tpan.at[side, pl.ds(0, W)] if k == TQ else dall.at[side]

    def sib_copy(k):
        return remote(spread(k, s), spread(k, s), sb_s.at[k], sb_r.at[k], sibling)

    def root_sib(k):
        return remote(a_hbm.at[pl.ds(k * ck, ck), cols(0)], spread(k, s), sb_s.at[k], sb_r.at[k], sibling)

    def sib_in(k):
        return remote(spread(k, 1 - s), spread(k, 1 - s), sb_s.at[k], sb_r.at[k], sibling)

    def forward(k):
        @pl.when(has_before)
        def _():
            chain_copy(k).wait_recv()

            @pl.when(has_after)
            def _():
                chain_copy(k).start()
            if k == DQ:
                for off in range(1, R):
                    da_copy(off).start()
            else:
                sib_copy(k).start()

    left = list(range(EARLY)) + [DQ] + list(range(EARLY, MIDDLE)) + [TQ] + list(range(MIDDLE, CHUNKS))

    def some(count):
        for _ in range(min(count, len(left))):
            forward(left.pop(0))

    def until(k):
        while k in left:
            some(1)

    def from_root(first, last):
        for k in range(first, last):
            @pl.when(has_after)
            def _():
                root_copy(k).start()
            root_sib(k).start()

    @pl.when(at_root)
    def _():
        from_root(0, EARLY)

    def gather(j):
        return select(sel_t[...], asw[:, j * nb:(j + 1) * nb])

    load(0).wait()
    first = gather(0)

    @pl.when(at_root)
    def _():
        dall[s, rows(r, W), :] = first

        @pl.when(has_after)
        def _():
            chain_copy(DQ).start()
        for off in range(1, R):
            da_copy(off).start()
        from_root(EARLY, MIDDLE)
        pan[s] = asw[:, 0:nb]

    @pl.when(has_before)
    def _():
        pall[0, rows(r, W), :] = first
        ag_start(0)

    def share(j):
        load(j).wait()
        pall[j, rows(r, W), :] = gather(j)
        ag_start(j)

    share(1)

    if W < nb:
        for j in range(NJ):
            tops[j, W:nb, :] = jnp.zeros((nb - W, nb), F32)
        for k in range(2):
            tpan[k, W:nb, :] = jnp.zeros((nb - W, nb), F32)

    @pl.when(is_top)
    def _():
        owner = jnp.where(r == 0, owners[0], owners[1])
        slot = jnp.where(r == 0, slots[0], slots[1])
        for q in range(R):
            aim = jnp.where(owner == q, slot, -1.0)
            split[q * cap:(q + 1) * cap, :] = jnp.where(
                jnp.broadcast_to(aim, (cap, nb)) == sub_f[0:cap], 1.0, 0.0).astype(BF16)
        tcomp[0] = select(split[...], asw[0:nb, 0:nb])

        @pl.when(at_root)
        def _():
            tpan[s, rows(top_half, cap), :] = tcomp[0, rows(r, cap), :]
            for off in range(1, R):
                tq_copy(off).start()

        @pl.when(has_before)
        def _():
            tops[0, rows(top_half, cap), :] = tcomp[0, rows(r, cap), :]
            for off in range(1, R):
                tz_copy(off).start()

    until(DQ)

    for j in range(2, NJ):
        share(j)
        ag_pass(j - 2)
        some(1)

    @pl.when(is_top)
    def _():
        for j in range(1, NJ):
            tcomp[j] = select(split[...], asw[0:nb, j * nb:(j + 1) * nb])
            tops[j, rows(top_half, cap), :] = tcomp[j, rows(r, cap), :]
        for off in range(1, R):
            to_copy(off).start()

    some(1)

    @pl.when(at_root)
    def _():
        from_tops(tq_in)

        @pl.when(has_after)
        def _():
            chain_copy(TQ).start()
        sib_copy(TQ).start()
        from_root(MIDDLE, CHUNKS)
        tops[0] = tpan[s]

    wide = tall.T
    for t in range(height // nb):
        spots = slice(t * nb, (t + 1) * nb)
        sel[spots, :] = jnp.where(wide == sub_f + float(t * nb), 1.0, 0.0).astype(BF16)
    for k in range(2):
        aim = owners[k].astype(F32) * float(W) + (slots[k] + float(k * cap))
        aim = jnp.broadcast_to(aim, (nb, nb)).T
        for t in range(R * W // nb):
            place[k * nb:(k + 1) * nb, t * nb:(t + 1) * nb] = jnp.where(
                aim == lane_f + float(t * nb), 1.0, 0.0).astype(BF16)
    some(1)
    for off in range(1, R):
        da_in(off).wait_recv()
    sib_copy(DQ).start()
    some(1)
    ag_pass(NJ - 2)
    ones = jnp.full((nb, nb), 1.0, BF16)

    @pl.loop(0, TILES)
    def _(t):
        spots = rows(t, height // TILES)
        hit[spots, :] = mm(sel[spots, :], ones)

    @pl.when(at_root)
    def _():
        pall[0] = dall[s]

    some(1)
    sib_in(DQ).wait_recv()
    for k in range(2):
        dh[k] = select(place[...], dall[k])
    upper00 = jnp.where(sub <= lane, exact(linv_ref[0], dh[0, 0:nb, :]), 0.0)
    some(1)
    ag_pass(NJ - 1)
    res[0] = upper_inverse(upper00, sub, lane)
    some(1)
    res[1] = exact(dh[0, nb:two, :], res[0])
    upper01 = exact(linv_ref[0], dh[1, 0:nb, :])
    rest = dh[1, nb:two, :] - exact(res[1], upper01)
    upper11 = jnp.where(sub <= lane, exact(linv_ref[1], rest), 0.0)
    res[2] = -exact(res[0], upper01)
    some(2)
    res[3] = upper_inverse(upper11, sub, lane)
    some(2)
    res[2] = exact(res[2], res[3])
    mixed = -exact(exact(linv_ref[1], res[1]), linv_ref[0])

    def spread_left(at, value):
        high, low = halves(value)
        return [mm(part, place[at * nb:(at + 1) * nb, :]) for part in (high, low)]

    me_hi[0:nb, :], me_lo[0:nb, :] = [v.astype(BF16) for v in spread_left(0, linv_ref[0])]
    below = [x + y for x, y in zip(spread_left(0, mixed), spread_left(1, linv_ref[1]))]
    me_hi[nb:two, :], me_lo[nb:two, :] = [v.astype(BF16) for v in below]
    some(1)

    inv0 = halves(res[0])
    cross = halves(res[2])
    inv1 = halves(res[3])

    def reduce_left(first, second):
        left0 = halves(first)
        left1 = halves(second)
        return dot3(left0, inv0), dot3(left0, cross) + dot3(left1, inv1)

    from_tops(to_in)

    @pl.when(has_before)
    def _():
        from_tops(tz_in)

    for j in range(NJ):
        spots = slice(j * nb, (j + 1) * nb)
        placed = select(sel[...], tops[j])
        asw[:, spots] = jnp.where(hit[...] > 0.5, placed, asw[:, spots])
        some(1)

    until(TQ)
    sib_in(TQ).wait_recv()
    low0, low1 = reduce_left(tpan[0], tpan[1])
    high, low = halves(jnp.concatenate([low0, low1], axis=1))
    lt_hi[...] = high
    lt_lo[...] = low
    some(1)

    for j in range(NJ):
        ag_finish(j)
        spots = slice(j * nb, (j + 1) * nb)
        value = dot3((me_hi[...], me_lo[...]), halves(pall[j]))
        u_f[:, spots] = value
        u_hi[:, spots], u_lo[:, spots] = halves(value)
        some(1)

    step = height // TILES

    def update(t, start):
        spots = pl.ds(start, step)
        low0, low1 = reduce_left(pan[0, spots, :], pan[1, spots, :])
        chosen = sel[spots, :]
        here = hit[spots, :] > 0.5
        moved = mm(chosen, lt_hi[...]) + mm(chosen, lt_lo[...])
        low0 = jnp.where(here, moved[:, 0:nb], low0)
        low1 = jnp.where(here, moved[:, nb:two], low1)
        high, low = halves(jnp.concatenate([low0, low1], axis=1))
        asw[spots, :] = asw[spots, :] - dot3((high, low), (u_hi[...], u_lo[...]))

        @pl.when(c == 0)
        def _():
            asw[spots, 0:nb] = low0

        @pl.when(c == 1)
        def _():
            asw[spots, 0:nb] = low1

    per_tile = CHUNKS // TILES
    for t in range(TILES):
        while left and left[0] < (t + 1) * per_tile:
            some(1)
        for k in range(t * per_tile, (t + 1) * per_tile):
            sib_in(k).wait_recv()
        update(t, t * step)
        if t == 0:
            @pl.when(r == 0)
            def _():
                asw[0:nb, :] = u_f[0:nb, :]

                @pl.when(c == 0)
                def _():
                    asw[0:nb, 0:nb] = jnp.where(sub <= lane, u_f[0:nb, 0:nb], 0.0)

            @pl.when(r == 1)
            def _():
                asw[0:nb, :] = u_f[nb:two, :]

                @pl.when(c == 0)
                def _():
                    asw[0:nb, 0:nb] = res[1]

                @pl.when(c == 1)
                def _():
                    asw[0:nb, 0:nb] = jnp.where(sub <= lane, u_f[nb:two, 0:nb], 0.0)

    for j in range(NJ):
        def gone(j=j):
            for i in range(R - 1):
                ag_copy(j, i).wait_send()
        past_root(j, gone)

    @pl.when(is_top)
    def _():
        for off in range(1, R):
            to_copy(off).wait_send()
            tq_copy(off).wait_send()

    for off in range(1, R):
        da_copy(off).wait_send()

    for k in range(CHUNKS + 2):
        sib_copy(k).wait_send()

        @pl.when(has_after)
        def _():
            chain_copy(k).wait_send()


def even_device(matrix, pivots, lower_inverse):
    R = lax.axis_size("row")
    C = lax.axis_size("col")
    height, width = matrix.shape
    nb = lower_inverse.shape[1]
    two = 2 * nb
    nj = width // nb
    cap = room(R, nb)
    dma = pltpu.SemaphoreType.DMA
    vm = pltpu.VMEM
    return pl.pallas_call(
        functools.partial(kernel, R, C, nb),
        out_shape=jax.ShapeDtypeStruct((height, width), F32),
        in_specs=[pl.BlockSpec(memory_space=pl.ANY)] + [pl.BlockSpec(memory_space=pltpu.VMEM)] * 2,
        out_specs=pl.BlockSpec(memory_space=pltpu.VMEM),
        scratch_shapes=[
            vm((height, nb), BF16), vm((2 * cap, height), BF16), vm((two, 2 * cap * R), BF16),
            vm((cap * R, nb), BF16), vm((nj, cap * R, nb), F32), vm((nj, 2 * cap * R, nb), F32),
            vm((2, 2 * cap * R, nb), F32), vm((nj, nb, nb), F32), vm((2, nb, nb), F32),
            vm((2, two, nb), F32), vm((2, height, nb), F32), vm((4, nb, nb), F32),
            vm((nb, two), BF16), vm((nb, two), BF16),
            vm((two, 2 * cap * R), BF16), vm((two, 2 * cap * R), BF16),
            vm((two, width), BF16), vm((two, width), BF16), vm((two, width), F32),
            vm((height, nb), F32),
            dma((nj,)), dma((R - 1,)), dma((2,)), dma((R - 1,)), dma((R - 1,)),
            dma((R - 1,)), dma((2,)),
            dma((nj * (R - 1),)), dma((nj * (R - 1),)),
            dma((CHUNKS + 2,)), dma((CHUNKS + 2,)), dma((CHUNKS + 2,)), dma((CHUNKS + 2,)),
        ],
        compiler_params=pltpu.CompilerParams(
            collective_id=0, has_side_effects=True, vmem_limit_bytes=50 * 1024 * 1024),
    )(matrix, pivots, lower_inverse)


def any_kernel(R, C, nb, a_hbm, piv_hbm, linv_hbm, asw,
           a_v, piv_ref, linv_ref, sel, sel_t, pm, pf, rsbuf, tops, tp, dpart, dbuf, dh, pan, res,
           u_hi, u_lo, u_f, hit,
           load_sem, piv_sem, linv_sem, d_s, d_r, tp_s, tp_r, rs_s, rs_r, ag_s, ag_r,
           to_s, to_r, ch_s, ch_r, sb_s, sb_r):
    height, width = a_v.shape
    two = 2 * nb
    ch = two // R
    ck = height // CHUNKS
    r = lax.axis_index("row")
    c = lax.axis_index("col")
    s = lax.rem(c, 2)
    sibling = {"col": c + 1 - 2 * s}

    load = pltpu.make_async_copy(a_hbm, a_v, load_sem)
    load_piv = pltpu.make_async_copy(piv_hbm, piv_ref, piv_sem)
    load_linv = pltpu.make_async_copy(linv_hbm, linv_ref, linv_sem)
    load_piv.start()
    load.start()
    load_linv.start()

    barrier = pltpu.get_barrier_semaphore()
    for off in range(1, R):
        pl.semaphore_signal(barrier, inc=1, device_id={"row": lax.rem(r + off, R)}, device_id_type=MESH)
    has_after = c + 2 < C
    has_before = c >= 2

    @pl.when(has_after)
    def _():
        pl.semaphore_signal(barrier, inc=1, device_id={"col": jnp.minimum(c + 2, C - 1)}, device_id_type=MESH)

    @pl.when(has_before)
    def _():
        pl.semaphore_signal(barrier, inc=1, device_id={"col": jnp.maximum(c - 2, 0)}, device_id_type=MESH)

    pl.semaphore_signal(barrier, inc=1, device_id=sibling, device_id_type=MESH)

    load_piv.wait()
    shift = nb.bit_length() - 1
    rshift = R.bit_length() - 1
    lane = lax.broadcasted_iota(jnp.int32, (nb, nb), 1)
    sub = lax.broadcasted_iota(jnp.int32, (nb, nb), 0)
    for k in range(2):
        p = piv_ref[k:k + 1, :]
        block = jnp.right_shift(p, shift)
        local = jnp.left_shift(jnp.right_shift(block, rshift), shift) + jnp.bitwise_and(p, nb - 1)
        local = jnp.where(jnp.bitwise_and(block, R - 1) == r, local, -1)
        wide = jnp.broadcast_to(local, (nb, nb))
        tall = wide.astype(F32).T
        for t in range(height // nb):
            spots = slice(t * nb, (t + 1) * nb)
            sel[spots, k * nb:(k + 1) * nb] = jnp.where(wide == sub + t * nb, 1.0, 0.0).astype(BF16)
            sel_t[k * nb:(k + 1) * nb, spots] = jnp.where(
                tall == (lane + t * nb).astype(F32), 1.0, 0.0).astype(BF16)

    load.wait()
    load_linv.wait()
    pl.semaphore_wait(barrier, R + jnp.minimum(c // 2, 1) + jnp.minimum((C - 1 - c) // 2, 1))

    def remote(src, dst, send, recv, where):
        return pltpu.make_async_remote_copy(
            src_ref=src, dst_ref=dst, send_sem=send, recv_sem=recv, device_id=where, device_id_type=MESH)

    def row_peer(off):
        return {"row": lax.rem(r + off, R)}

    def tp_copy(off):
        q = jnp.minimum(r, 1)
        return remote(a_v.at[0:nb, 0:nb], tp.at[pl.ds(pl.multiple_of(q * nb, nb), nb)],
                      tp_s.at[off - 1], tp_r.at[q], row_peer(off))

    def tops_copy(off):
        q = jnp.minimum(r, 1)
        return remote(a_v.at[0:nb], tops.at[pl.ds(pl.multiple_of(q * nb, nb), nb)],
                      to_s.at[off - 1], to_r.at[q], row_peer(off))

    def d_copy(off):
        return remote(dpart, dbuf.at[off - 1], d_s.at[off - 1], d_r.at[off - 1], row_peer(off))

    def rs_copy(off):
        to = lax.rem(r + off, R)
        return remote(pm.at[pl.ds(pl.multiple_of(to * ch, ch), ch)], rsbuf.at[off - 1],
                      rs_s.at[off - 1], rs_r.at[off - 1], {"row": to})

    def ag_copy(off):
        mine = pf.at[pl.ds(pl.multiple_of(r * ch, ch), ch)]
        return remote(mine, mine, ag_s.at[off - 1], ag_r.at[off - 1], row_peer(off))

    def ag_in(off):
        src = lax.rem(r - off + R, R)
        there = pf.at[pl.ds(pl.multiple_of(src * ch, ch), ch)]
        return remote(there, there, ag_s.at[off - 1], ag_r.at[off - 1], row_peer(off))

    def piece(side, k):
        if k < CHUNKS:
            return pan.at[side, pl.ds(k * ck, ck)]
        return dh.at[side, pl.ds((k - CHUNKS) * nb, nb)]

    def chain_copy(k):
        part = piece(s, k)
        return remote(part, part, ch_s.at[k], ch_r.at[k], {"col": jnp.minimum(c + 2, C - 2 + s)})

    def sib_copy(k):
        part = piece(s, k)
        return remote(part, part, sb_s.at[k], sb_r.at[k], sibling)

    def sib_in(k):
        part = piece(1 - s, k)
        return remote(part, part, sb_s.at[k], sb_r.at[k], sibling)

    is_top = r < 2
    at_root = c < 2

    @pl.when(at_root)
    def _():
        @pl.when(is_top)
        def _():
            for off in range(1, R):
                tp_copy(off).start()
            tp[pl.ds(pl.multiple_of(jnp.minimum(r, 1) * nb, nb), nb), :] = a_v[0:nb, 0:nb]

        dpart[...] = select(sel_t[...], a_v[:, 0:nb])
        for off in range(1, R):
            d_copy(off).start()

    ones = jnp.full((two, nb), 1.0, BF16)

    @pl.loop(0, TILES)
    def _(t):
        spots = pl.ds(pl.multiple_of(t * (height // TILES), height // TILES), height // TILES)
        hit[spots, :] = mm(sel[spots, :], ones)

    def panel(first, last):
        high, middle, low = thirds(tp[...])
        for k in range(first, last):
            spots = slice(k * ck, (k + 1) * ck)
            chosen = sel[spots, :]
            placed = mm(chosen, high) + (mm(chosen, middle) + mm(chosen, low))
            pan[s, spots, :] = jnp.where(hit[spots, :] > 0.5, placed, a_v[spots, 0:nb])
            chain_copy(k).start()
            sib_copy(k).start()

    @pl.loop(0, width // nb)
    def _(t):
        spots = pl.ds(pl.multiple_of(t * nb, nb), nb)
        pm[:, spots] = select(sel_t[...], a_v[:, spots])

    @pl.when(at_root)
    def _():
        for q in range(2):
            @pl.when(r != q)
            def _():
                part = tp.at[q * nb:(q + 1) * nb]
                remote(part, part, tp_s.at[0], tp_r.at[q], row_peer(1)).wait_recv()
        panel(0, ANY_EARLY)

    for off in range(1, R):
        rs_copy(off).start()

    @pl.when(is_top)
    def _():
        for off in range(1, R):
            tops_copy(off).start()
        tops[pl.ds(pl.multiple_of(jnp.minimum(r, 1) * nb, nb), nb), :] = a_v[0:nb, :]

    @pl.when(at_root)
    def _():
        total = dpart[...]
        for off in range(1, R):
            d_copy(off).wait_recv()
            total = total + dbuf[off - 1]
        dh[s] = total
        for k in range(CHUNKS, CHUNKS + 2):
            chain_copy(k).start()
            sib_copy(k).start()
        panel(ANY_EARLY, CHUNKS)

    def forward(k):
        @pl.when(c >= 2)
        def _():
            chain_copy(k).wait_recv()

            @pl.when(c + 2 < C)
            def _():
                chain_copy(k).start()
            sib_copy(k).start()

    for k in range(ANY_EARLY):
        forward(k)
    forward(CHUNKS)
    forward(CHUNKS + 1)

    own = pl.ds(pl.multiple_of(r * ch, ch), ch)
    total = pm[own, :]
    for off in range(1, R):
        rs_copy(off).wait_recv()
        total = total + rsbuf[off - 1]
    pf[own, :] = total
    for off in range(1, R):
        ag_copy(off).start()

    left = list(range(ANY_EARLY, CHUNKS))

    def some(count):
        for _ in range(min(count, len(left))):
            forward(left.pop(0))

    sib_in(CHUNKS).wait_recv()
    sib_in(CHUNKS + 1).wait_recv()
    upper00 = jnp.where(sub <= lane, exact(linv_ref[0], dh[0, 0:nb, :]), 0.0)
    res[0] = upper_inverse(upper00, sub, lane)
    some(1)
    res[1] = exact(dh[0, nb:two, :], res[0])
    upper01 = exact(linv_ref[0], dh[1, 0:nb, :])
    rest = dh[1, nb:two, :] - exact(res[1], upper01)
    upper11 = jnp.where(sub <= lane, exact(linv_ref[1], rest), 0.0)
    res[2] = -exact(res[0], upper01)
    some(1)
    res[3] = upper_inverse(upper11, sub, lane)
    some(2)
    res[2] = exact(res[2], res[3])
    mixed = -exact(exact(linv_ref[1], res[1]), linv_ref[0])
    some(1)

    for q in range(2):
        @pl.when(r != q)
        def _():
            part = tops.at[q * nb:(q + 1) * nb]
            remote(part, part, to_s.at[0], to_r.at[q], row_peer(1)).wait_recv()

    for t in range(width // nb):
        spots = slice(t * nb, (t + 1) * nb)
        placed = select(sel[...], tops[:, spots])
        asw[:, spots] = jnp.where(hit[...] > 0.5, placed, a_v[:, spots])
        some(1)

    for off in range(1, R):
        ag_in(off).wait_recv()

    inv_low0 = linv_ref[0]
    inv_low1 = linv_ref[1]
    u_f[0:nb, :] = dot3(halves(inv_low0), halves(pf[0:nb, :]))
    u_f[nb:two, :] = (dot3(halves(mixed), halves(pf[0:nb, :]))
                      + dot3(halves(inv_low1), halves(pf[nb:two, :])))
    high, low = halves(u_f[...])
    u_hi[...] = high
    u_lo[...] = low

    step = height // TILES
    inv0 = halves(res[0])
    cross = halves(res[2])
    inv1 = halves(res[3])

    def update(t, start):
        spots = pl.ds(start, step)
        left0 = halves(pan[0, spots, :])
        left1 = halves(pan[1, spots, :])
        low0 = dot3(left0, inv0)
        low1 = dot3(left0, cross) + dot3(left1, inv1)
        high, low = halves(jnp.concatenate([low0, low1], axis=1))
        asw[spots, :] = asw[spots, :] - dot3((high, low), (u_hi[...], u_lo[...]))

        @pl.when(c == 0)
        def _():
            asw[spots, 0:nb] = low0

        @pl.when(c == 1)
        def _():
            asw[spots, 0:nb] = low1

    per_tile = CHUNKS // TILES
    for t in range(TILES):
        some(1)
        while left and left[0] < (t + 1) * per_tile:
            some(1)
        for k in range(t * per_tile, (t + 1) * per_tile):
            sib_in(k).wait_recv()
        update(t, t * step)
        if t == 0:
            @pl.when(r == 0)
            def _():
                asw[0:nb, :] = u_f[0:nb, :]

                @pl.when(c == 0)
                def _():
                    asw[0:nb, 0:nb] = jnp.where(sub <= lane, u_f[0:nb, 0:nb], 0.0)

            @pl.when(r == 1)
            def _():
                asw[0:nb, :] = u_f[nb:two, :]

                @pl.when(c == 0)
                def _():
                    asw[0:nb, 0:nb] = res[1]

                @pl.when(c == 1)
                def _():
                    asw[0:nb, 0:nb] = jnp.where(sub <= lane, u_f[nb:two, 0:nb], 0.0)

    for off in range(1, R):
        rs_copy(off).wait_send()
        ag_copy(off).wait_send()

    @pl.when(is_top)
    def _():
        for off in range(1, R):
            tops_copy(off).wait_send()

        @pl.when(at_root)
        def _():
            for off in range(1, R):
                tp_copy(off).wait_send()

    for k in range(CHUNKS + 2):
        sib_copy(k).wait_send()

        @pl.when(c + 2 < C)
        def _():
            chain_copy(k).wait_send()

    @pl.when(at_root)
    def _():
        for off in range(1, R):
            d_copy(off).wait_send()


def any_device(matrix, pivots, lower_inverse):
    R = lax.axis_size("row")
    C = lax.axis_size("col")
    height, width = matrix.shape
    nb = lower_inverse.shape[1]
    two = 2 * nb
    dma = pltpu.SemaphoreType.DMA
    vm = pltpu.VMEM
    return pl.pallas_call(
        functools.partial(any_kernel, R, C, nb),
        out_shape=jax.ShapeDtypeStruct((height, width), F32),
        in_specs=[pl.BlockSpec(memory_space=pl.ANY)] * 3,
        out_specs=pl.BlockSpec(memory_space=pltpu.VMEM),
        scratch_shapes=[
            vm((height, width), F32), vm((2, nb), jnp.int32), vm((2, nb, nb), F32),
            vm((height, two), BF16), vm((two, height), BF16),
            vm((two, width), F32), vm((two, width), F32),
            vm((R - 1, two // R, width), F32), vm((two, width), F32),
            vm((two, nb), F32), vm((two, nb), F32), vm((R - 1, two, nb), F32),
            vm((2, two, nb), F32), vm((2, height, nb), F32), vm((4, nb, nb), F32),
            vm((two, width), BF16), vm((two, width), BF16), vm((two, width), F32),
            vm((height, nb), F32),
            dma, dma, dma, dma((R - 1,)), dma((R - 1,)), dma((R - 1,)), dma((2,)),
            dma((R - 1,)), dma((R - 1,)), dma((R - 1,)), dma((R - 1,)),
            dma((R - 1,)), dma((2,)), dma((CHUNKS + 2,)), dma((CHUNKS + 2,)),
            dma((CHUNKS + 2,)), dma((CHUNKS + 2,)),
        ],
        compiler_params=pltpu.CompilerParams(
            collective_id=1, has_side_effects=True, vmem_limit_bytes=50 * 1024 * 1024),
    )(matrix, pivots, lower_inverse)


def most_kernel(R, nb, piv_ref, out_ref):
    owner = jnp.bitwise_and(jnp.right_shift(piv_ref[...], nb.bit_length() - 1), R - 1)
    most = jnp.zeros((2, 1), F32)
    for q in range(R):
        most = jnp.maximum(most, jnp.sum(jnp.where(owner == q, 1.0, 0.0), axis=1, keepdims=True))
    out_ref[0] = jnp.max(most).astype(jnp.int32)


def on_device(matrix, pivots, lower_inverse):
    R = lax.axis_size("row")
    nb = lower_inverse.shape[1]
    most = pl.pallas_call(
        functools.partial(most_kernel, R, nb),
        out_shape=jax.ShapeDtypeStruct((1,), jnp.int32),
        in_specs=[pl.BlockSpec(memory_space=pltpu.VMEM)],
        out_specs=pl.BlockSpec(memory_space=pltpu.SMEM),
    )(pivots)
    return lax.cond(most[0] <= room(R, nb), even_device, any_device, matrix, pivots, lower_inverse)


def solution(mesh):
    return jax.shard_map(
        on_device,
        mesh=mesh,
        in_specs=(P("row", "col"), P(), P()),
        out_specs=P("row", "col"),
        check_vma=False,
    )
```

```python
import functools

import jax
import jax.numpy as jnp
from jax import lax
from jax.experimental import pallas as pl
from jax.experimental.pallas import tpu as pltpu
from jax.sharding import PartitionSpec as P

MESH = pl.DeviceIdType.MESH
F32 = jnp.float32
BF16 = jnp.bfloat16
CHUNKS = 16
EARLY = 1
MIDDLE = 9
ANY_EARLY = 3
FAR = 4
TILES = 4


def mm(left, right):
    return jnp.dot(left, right, preferred_element_type=F32)


def exact(left, right):
    return jnp.dot(left, right, precision=lax.Precision.HIGHEST, preferred_element_type=F32)


def halves(value):
    high = value.astype(BF16)
    return high, (value - high.astype(F32)).astype(BF16)


def thirds(value):
    high = value.astype(BF16)
    rest = value - high.astype(F32)
    middle = rest.astype(BF16)
    return high, middle, (rest - middle.astype(F32)).astype(BF16)


def select(chosen, value):
    high, middle, low = thirds(value)
    return mm(chosen, high) + (mm(chosen, middle) + mm(chosen, low))


def dot3(left, right):
    left_high, left_low = left
    right_high, right_low = right
    return mm(left_high, right_high) + (mm(left_low, right_high) + mm(left_high, right_low))


def upper_inverse(upper, rows, cols):
    on_diag = rows == cols
    eye = jnp.where(on_diag, 1.0, 0.0)
    kept = jnp.where(on_diag, upper, 0.0)
    scaled = upper / jnp.sum(kept, axis=1, keepdims=True)
    power = jnp.where(rows < cols, -scaled, 0.0)
    result = eye + power
    reach = 2
    while reach < upper.shape[0]:
        power = exact(power, power)
        result = result + exact(result, power)
        reach = reach * 2
    return result / jnp.sum(kept, axis=0, keepdims=True)


def select2(chosen, value):
    high, low = halves(value)
    return mm(chosen, high) + mm(chosen, low)


def close(left, right):
    left_high, left_low = halves(left)
    right_high, right_low = halves(right)
    return mm(jnp.concatenate([left_high, left_low, left_high], axis=1),
              jnp.concatenate([right_high, right_high, right_low], axis=0))


def quick_inverse(upper, rows, cols, between):
    on_diag = rows == cols
    eye = jnp.where(on_diag, 1.0, 0.0)
    kept = jnp.where(on_diag, upper, 0.0)
    scaled = upper / jnp.sum(kept, axis=1, keepdims=True)
    power = jnp.where(rows < cols, -scaled, 0.0)
    result = eye + power
    reach = 2
    while reach < upper.shape[0]:
        power = close(power, power)
        result = result + close(result, power)
        reach = reach * 2
        if reach in (8, 32):
            between(1)
    return result / jnp.sum(kept, axis=0, keepdims=True)


def room(R, nb):
    return (nb // R + 31) // 16 * 16


def kernel(R, C, nb, a_hbm, piv_ref, linv_ref, asw,
           sel, sel_t, place, split, tcomp, pall, dall, tops, tpan, dh, pan, res, lt, inv3, me3, w3, tw, u_f, hit,
           load_sem, tq_s, tq_r, da_s, da_r, to_s, to_r,
           ag_s, ag_r, ch_s, ch_r, sb_s, sb_r):
    height, width = asw.shape
    two = 2 * nb
    cap = room(R, nb)
    W = 2 * cap
    ck = height // CHUNKS
    NJ = width // nb
    r = lax.axis_index("row")
    c = lax.axis_index("col")
    s = lax.rem(c, 2)
    sibling = {"col": c + 1 - 2 * s}
    top_half = jnp.minimum(r, 1)
    odd = lax.rem(r, 2)
    relay = R == 4

    def flip(bit):
        if bit == 1:
            return r + 1 - 2 * odd
        if bit == 2:
            return lax.rem(r + 2, 4)
        return 3 - r

    def cols(j):
        return pl.ds(j * nb, nb)

    def load(j):
        return pltpu.make_async_copy(a_hbm.at[:, cols(j)], asw.at[:, cols(j)], load_sem.at[j])

    for j in range(NJ):
        load(j).start()

    has_after = c + 2 < C
    has_before = c >= 2
    at_root = c < 2
    is_top = r < 2

    barrier = pltpu.get_barrier_semaphore()
    for off in range(1, R):
        pl.semaphore_signal(barrier, inc=1, device_id={"row": lax.rem(r + off, R)}, device_id_type=MESH)

    @pl.when(has_after)
    def _():
        pl.semaphore_signal(barrier, inc=1, device_id={"col": jnp.minimum(c + 2, C - 1)}, device_id_type=MESH)

    @pl.when(has_before)
    def _():
        pl.semaphore_signal(barrier, inc=1, device_id={"col": jnp.maximum(c - 2, 0)}, device_id_type=MESH)

    pl.semaphore_signal(barrier, inc=1, device_id=sibling, device_id_type=MESH)

    pl.semaphore_wait(barrier, R + jnp.minimum(c // 2, 1) + jnp.minimum((C - 1 - c) // 2, 1))

    def remote(src, dst, send, recv, where):
        return pltpu.make_async_remote_copy(
            src_ref=src, dst_ref=dst, send_sem=send, recv_sem=recv, device_id=where, device_id_type=MESH)

    def rows(index, count):
        return pl.ds(pl.multiple_of(index * count, count), count)

    def peer(off):
        return lax.rem(r + off, R)

    def origin(off):
        return lax.rem(r - off + R, R)

    def da_copy(off):
        part = dall.at[s, rows(r, W)]
        return remote(part, part, da_s.at[off - 1], da_r.at[off - 1], {"row": peer(off)})

    def da_in(off):
        part = dall.at[s, rows(origin(off), W)]
        return remote(part, part, da_s.at[off - 1], da_r.at[off - 1], {"row": peer(off)})

    def tq_copy(off):
        return remote(tcomp.at[0, rows(peer(off), cap)], tpan.at[s, rows(top_half, cap)],
                      tq_s.at[off - 1], tq_r.at[top_half], {"row": peer(off)})

    def tz_copy(off):
        return remote(tcomp.at[0, rows(peer(off), cap)], tops.at[0, rows(top_half, cap)],
                      tq_s.at[off - 1], tq_r.at[top_half], {"row": peer(off)})

    def to_copy(off):
        return remote(tcomp.at[pl.ds(1, NJ - 1), rows(peer(off), cap)],
                      tops.at[pl.ds(1, NJ - 1), rows(top_half, cap)],
                      to_s.at[off - 1], to_r.at[top_half], {"row": peer(off)})

    def tq_in(half):
        part = tpan.at[s, pl.ds(half * cap, cap)]
        return remote(part, part, tq_s.at[0], tq_r.at[half], {"row": peer(1)})

    def tz_in(half):
        part = tops.at[0, pl.ds(half * cap, cap)]
        return remote(part, part, tq_s.at[0], tq_r.at[half], {"row": peer(1)})

    def to_in(half):
        part = tops.at[pl.ds(1, NJ - 1), pl.ds(half * cap, cap)]
        return remote(part, part, to_s.at[0], to_r.at[half], {"row": peer(1)})

    def from_tops(copy):
        for half in range(2):
            @pl.when(r != half)
            def _():
                copy(half).wait_recv()

    def ag_copy(j, i):
        at = j * (R - 1) + i
        if not relay:
            part = pall.at[j, rows(r, W)]
            return remote(part, part, ag_s.at[at], ag_r.at[at], {"row": peer(i + 1)})
        if i < 2:
            part = pall.at[j, rows(r, W)]
            return remote(part, part, ag_s.at[at], ag_r.at[at], {"row": flip(i + 1)})
        bit = 1 + j % 2
        part = pall.at[j, rows(flip(3 - bit), W)]
        return remote(part, part, ag_s.at[at], ag_r.at[at], {"row": flip(bit)})

    def ag_in(j, i):
        at = j * (R - 1) + i
        src = flip(i + 1) if relay else origin(i + 1)
        part = pall.at[j, rows(src, W)]
        return remote(part, part, ag_s.at[at], ag_r.at[at], {"row": peer(1)})

    def ag_start(j):
        for i in range(2 if relay else R - 1):
            ag_copy(j, i).start()

    def ag_relay_from(j):
        return 1 - j % 2

    def past_root(j, go):
        if j == 0:
            pl.when(has_before)(go)
        else:
            go()

    def ag_pass(j):
        if relay:
            def go():
                ag_in(j, ag_relay_from(j)).wait_recv()
                ag_copy(j, 2).start()
            past_root(j, go)

    def ag_finish(j):
        def go():
            for i in range(R - 1):
                if not (relay and i == ag_relay_from(j)):
                    ag_in(j, i).wait_recv()
        past_root(j, go)

    TQ, DQ = CHUNKS, CHUNKS + 1

    def piece(k):
        if k < CHUNKS:
            return pan.at[s, pl.ds(k * ck, ck)]
        if k == TQ:
            return tpan.at[s, pl.ds(0, W)]
        return dall.at[s, rows(r, W)]

    after = {"col": jnp.minimum(c + 2, C - 2 + s)}

    def chain_copy(k):
        return remote(piece(k), piece(k), ch_s.at[k], ch_r.at[k], after)

    def root_copy(k):
        return remote(a_hbm.at[pl.ds(k * ck, ck), cols(0)], piece(k), ch_s.at[k], ch_r.at[k], after)

    def spread(k, side):
        if k < CHUNKS:
            return pan.at[side, pl.ds(k * ck, ck)]
        return tpan.at[side, pl.ds(0, W)] if k == TQ else dall.at[side]

    def sib_copy(k):
        return remote(spread(k, s), spread(k, s), sb_s.at[k], sb_r.at[k], sibling)

    def root_sib(k):
        return remote(a_hbm.at[pl.ds(k * ck, ck), cols(0)], spread(k, s), sb_s.at[k], sb_r.at[k], sibling)

    def sib_in(k):
        return remote(spread(k, 1 - s), spread(k, 1 - s), sb_s.at[k], sb_r.at[k], sibling)

    def forward(k):
        @pl.when(has_before)
        def _():
            chain_copy(k).wait_recv()

            @pl.when(has_after)
            def _():
                chain_copy(k).start()
            if k == DQ:
                for off in range(1, R):
                    da_copy(off).start()
            else:
                sib_copy(k).start()

    left = list(range(EARLY)) + [DQ] + list(range(EARLY, MIDDLE)) + [TQ] + list(range(MIDDLE, CHUNKS))

    def some(count):
        for _ in range(min(count, len(left))):
            forward(left.pop(0))

    def until(k):
        while k in left:
            some(1)

    def from_root(first, last):
        for k in range(first, last):
            @pl.when(has_after)
            def _():
                root_copy(k).start()
            root_sib(k).start()

    @pl.when(at_root)
    def _():
        from_root(0, EARLY)

    shift = nb.bit_length() - 1
    rshift = R.bit_length() - 1
    lane = lax.broadcasted_iota(jnp.int32, (nb, nb), 1)
    sub = lax.broadcasted_iota(jnp.int32, (nb, nb), 0)
    lane_f = lane.astype(F32)
    sub_f = sub.astype(F32)
    before = jnp.where(sub < lane, 1.0, 0.0).astype(BF16)
    owners, slots, talls = [], [], []
    for k in range(2):
        p = piv_ref[k:k + 1, :]
        block = jnp.right_shift(p, shift)
        owner = jnp.bitwise_and(block, R - 1)
        local = jnp.left_shift(jnp.right_shift(block, rshift), shift) + jnp.bitwise_and(p, nb - 1)
        hot = jnp.where(jnp.broadcast_to(owner, (16, nb)) == sub[0:16], 1.0, 0.0)
        rank = mm(hot.astype(BF16), before)
        slot = jnp.sum(hot * rank, axis=0, keepdims=True)
        mine = jnp.where(owner == r, slot, -1.0)
        match = jnp.broadcast_to(mine, (cap, nb)) == sub_f[0:cap]
        value = jnp.broadcast_to(local.astype(F32) + 1.0, (cap, nb))
        spot = jnp.sum(jnp.where(match, value, 0.0), axis=1, keepdims=True) - 1.0
        owners.append(owner)
        slots.append(slot)
        talls.append(jnp.broadcast_to(spot, (cap, nb)))
    if W < nb:
        talls.append(jnp.full((nb - W, nb), -1.0, F32))
    tall = jnp.concatenate(talls, axis=0)
    for t in range(height // nb):
        spots = slice(t * nb, (t + 1) * nb)
        sel_t[:, spots] = jnp.where(tall[0:W] == lane_f[0:W] + float(t * nb), 1.0, 0.0).astype(BF16)

    load(0).wait()
    first = select(sel_t[...], asw[:, 0:nb])

    @pl.when(at_root)
    def _():
        dall[s, rows(r, W), :] = first

        @pl.when(has_after)
        def _():
            chain_copy(DQ).start()
        for off in range(1, R):
            da_copy(off).start()
        from_root(EARLY, MIDDLE)
        pan[s] = asw[:, 0:nb]

    @pl.when(has_before)
    def _():
        pall[0, rows(r, W), :] = first
        ag_start(0)

    def collect(start, stop):
        value = select2(sel_t[...], asw[:, start * nb:stop * nb])
        for j in range(start, stop):
            pall[j, rows(r, W), :] = value[:, (j - start) * nb:(j - start + 1) * nb]

    load(1).wait()
    collect(1, 2)
    for j in range(2, NJ):
        load(j).wait()
    for j in range(2, NJ, 2):
        collect(j, min(j + 2, NJ))

    @pl.when(c >= FAR)
    def _():
        for j in range(1, NJ):
            ag_start(j)

    if W < nb:
        for j in range(NJ):
            tops[j, W:nb, :] = jnp.zeros((nb - W, nb), F32)
        for k in range(2):
            tpan[k, W:nb, :] = jnp.zeros((nb - W, nb), F32)
    wide = tall.T
    for t in range(height // nb):
        spots = slice(t * nb, (t + 1) * nb)
        value = jnp.where(wide == sub_f + float(t * nb), 1.0, 0.0).astype(BF16)
        sel[spots, 0:nb] = value
        sel[spots, nb:two] = value
    for k in range(2):
        aim = owners[k].astype(F32) * float(W) + (slots[k] + float(k * cap))
        aim = jnp.broadcast_to(aim, (nb, nb)).T
        for t in range(R * W // nb):
            place[k * nb:(k + 1) * nb, t * nb:(t + 1) * nb] = jnp.where(
                aim == lane_f + float(t * nb), 1.0, 0.0).astype(BF16)

    until(DQ)

    @pl.when(c < FAR)
    def _():
        for j in range(1, NJ):
            ag_start(j)

    @pl.when(is_top)
    def _():
        owner = jnp.where(r == 0, owners[0], owners[1])
        slot = jnp.where(r == 0, slots[0], slots[1])
        for q in range(R):
            aim = jnp.where(owner == q, slot, -1.0)
            aim = jnp.where(jnp.broadcast_to(aim, (cap, nb)) == sub_f[0:cap], 1.0, 0.0).astype(BF16)
            split[q * cap:(q + 1) * cap, 0:nb] = aim
            split[q * cap:(q + 1) * cap, nb:two] = aim
        value = mm(split[...], jnp.concatenate(halves(asw[0:nb, :]), axis=0))
        for j in range(NJ):
            tcomp[j] = value[:, j * nb:(j + 1) * nb]
        own = jnp.where(r == 0, value[0:cap, :], value[cap:2 * cap, :])

        @pl.when(at_root)
        def _():
            tpan[s, rows(top_half, cap), :] = own[:, 0:nb]
            for off in range(1, R):
                tq_copy(off).start()

        @pl.when(has_before)
        def _():
            tops[0, rows(top_half, cap), :] = own[:, 0:nb]
            for off in range(1, R):
                tz_copy(off).start()

        for off in range(1, R):
            to_copy(off).start()
        for j in range(1, NJ):
            tops[j, rows(top_half, cap), :] = own[:, j * nb:(j + 1) * nb]

    some(1)
    ones = jnp.full((two, nb), 1.0, BF16)

    @pl.loop(0, TILES)
    def _(t):
        spots = rows(t, height // TILES)
        hit[spots, :] = mm(sel[spots, :], ones)

    some(2)
    ag_pass(0)
    for off in range(1, R):
        da_in(off).wait_recv()
    sib_copy(DQ).start()

    @pl.when(at_root)
    def _():
        from_tops(tq_in)

        @pl.when(has_after)
        def _():
            chain_copy(TQ).start()
        sib_copy(TQ).start()
        from_root(MIDDLE, CHUNKS)
        tops[0] = tpan[s]
        pall[0] = dall[s]

    some(1)
    sib_in(DQ).wait_recv()
    both = select(place[...], jnp.concatenate([dall[0], dall[1]], axis=1))
    dh[0] = both[:, 0:nb]
    dh[1] = both[:, nb:two]
    upper00 = jnp.where(sub <= lane, exact(linv_ref[0], dh[0, 0:nb, :]), 0.0)
    upper01 = exact(linv_ref[0], dh[1, 0:nb, :])
    some(1)
    ag_pass(1)
    res[0] = quick_inverse(upper00, sub, lane, some)
    some(1)
    ag_pass(2)
    res[1] = exact(dh[0, nb:two, :], res[0])
    rest = dh[1, nb:two, :] - exact(res[1], upper01)
    upper11 = jnp.where(sub <= lane, exact(linv_ref[1], rest), 0.0)
    res[2] = -close(res[0], upper01)
    mixed = -close(close(linv_ref[1], res[1]), linv_ref[0])
    blank = jnp.zeros((nb, nb), F32)
    high, low = halves(jnp.concatenate([
        jnp.concatenate([linv_ref[0], blank], axis=1),
        jnp.concatenate([mixed, linv_ref[1]], axis=1)], axis=0))
    span = R * W
    high = mm(high, place[...]).astype(BF16)
    me3[:, 0:span] = high
    me3[:, span:2 * span] = mm(low, place[...]).astype(BF16)
    me3[:, 2 * span:3 * span] = high
    some(1)
    ag_pass(3)
    res[3] = quick_inverse(upper11, sub, lane, some)
    for j in range(4, NJ):
        ag_pass(j)
    some(1)

    def stack(value):
        high, low = halves(value)
        return jnp.concatenate([high, high, low], axis=0)

    def row_stack(value):
        high, low = halves(value)
        return jnp.concatenate([high, low, high], axis=1)

    inverse = jnp.concatenate([
        jnp.concatenate([res[0], close(res[2], res[3])], axis=1),
        jnp.concatenate([blank, res[3]], axis=1)], axis=0)
    inv3[...] = stack(inverse)
    left3 = row_stack(inverse)
    for j in range(0, NJ, 2):
        ag_finish(j)
        ag_finish(j + 1)
        spots = slice(j * nb, (j + 2) * nb)
        value = mm(me3[...], stack(jnp.concatenate([pall[j], pall[j + 1]], axis=1)))
        u_f[:, spots] = value
        w3[:, spots] = stack(mm(left3, stack(value)))
        some(1)

    until(TQ)
    sib_in(TQ).wait_recv()
    from_tops(to_in)

    @pl.when(has_before)
    def _():
        from_tops(tz_in)

    tp = row_stack(jnp.concatenate([tpan[0], tpan[1]], axis=1))
    swapped = jnp.concatenate([tops[j] for j in range(NJ)], axis=1) - mm(tp, w3[...])
    high, low = halves(swapped)
    tw[0:nb, :] = high
    tw[nb:two, :] = low

    @pl.when(at_root)
    def _():
        high, low = halves(mm(tp, inv3[...]))
        lt[0:nb, :] = high
        lt[nb:two, :] = low

    some(1)

    def update(start, count):
        spots = slice(start, start + count)
        here = hit[spots, :] > 0.5
        kept = row_stack(jnp.concatenate([
            jnp.where(here, 0.0, pan[0, spots, :]), jnp.where(here, 0.0, pan[1, spots, :])], axis=1))
        change = mm(kept, w3[...])
        moved = mm(sel[spots, :], tw[...])
        for j in range(NJ):
            part = slice(j * nb, (j + 1) * nb)
            asw[spots, part] = jnp.where(here, moved[:, part], asw[spots, part]) - change[:, part]

        @pl.when(at_root)
        def _():
            value = mm(kept, inv3[...]) + mm(sel[spots, :], lt[...])
            asw[spots, 0:nb] = jnp.where(c == 0, value[:, 0:nb], value[:, nb:two])

    step = height // TILES
    tiles = [(t * step, step) for t in range(TILES - 1)]
    tiles += [(height - step, step // 2), (height - step // 2, step // 2)]
    for start, count in tiles:
        while left and left[0] * ck < start + count:
            some(1)
        for k in range(start // ck, (start + count) // ck):
            sib_in(k).wait_recv()
        update(start, count)
        some(1)
        if start == 0:
            @pl.when(r == 0)
            def _():
                asw[0:nb, :] = u_f[0:nb, :]

                @pl.when(c == 0)
                def _():
                    asw[0:nb, 0:nb] = jnp.where(sub <= lane, u_f[0:nb, 0:nb], 0.0)

            @pl.when(r == 1)
            def _():
                asw[0:nb, :] = u_f[nb:two, :]

                @pl.when(c == 0)
                def _():
                    asw[0:nb, 0:nb] = res[1]

                @pl.when(c == 1)
                def _():
                    asw[0:nb, 0:nb] = jnp.where(sub <= lane, u_f[nb:two, 0:nb], 0.0)

    for j in range(NJ):
        def gone(j=j):
            for i in range(R - 1):
                ag_copy(j, i).wait_send()
        past_root(j, gone)

    @pl.when(is_top)
    def _():
        for off in range(1, R):
            to_copy(off).wait_send()
            tq_copy(off).wait_send()

    for off in range(1, R):
        da_copy(off).wait_send()

    for k in range(CHUNKS + 2):
        sib_copy(k).wait_send()

        @pl.when(has_after)
        def _():
            chain_copy(k).wait_send()


def even_device(matrix, pivots, lower_inverse):
    R = lax.axis_size("row")
    C = lax.axis_size("col")
    height, width = matrix.shape
    nb = lower_inverse.shape[1]
    two = 2 * nb
    nj = width // nb
    cap = room(R, nb)
    dma = pltpu.SemaphoreType.DMA
    vm = pltpu.VMEM
    return pl.pallas_call(
        functools.partial(kernel, R, C, nb),
        out_shape=jax.ShapeDtypeStruct((height, width), F32),
        in_specs=[pl.BlockSpec(memory_space=pl.ANY)] + [pl.BlockSpec(memory_space=pltpu.VMEM)] * 2,
        out_specs=pl.BlockSpec(memory_space=pltpu.VMEM),
        scratch_shapes=[
            vm((height, two), BF16), vm((2 * cap, height), BF16), vm((two, 2 * cap * R), BF16),
            vm((cap * R, two), BF16), vm((nj, cap * R, nb), F32), vm((nj, 2 * cap * R, nb), F32),
            vm((2, 2 * cap * R, nb), F32), vm((nj, nb, nb), F32), vm((2, nb, nb), F32),
            vm((2, two, nb), F32), vm((2, height, nb), F32), vm((4, nb, nb), F32),
            vm((two, two), BF16), vm((3 * two, two), BF16), vm((two, 6 * cap * R), BF16),
            vm((3 * two, width), BF16), vm((two, width), BF16), vm((two, width), F32),
            vm((height, nb), F32),
            dma((nj,)), dma((R - 1,)), dma((2,)), dma((R - 1,)), dma((R - 1,)),
            dma((R - 1,)), dma((2,)),
            dma((nj * (R - 1),)), dma((nj * (R - 1),)),
            dma((CHUNKS + 2,)), dma((CHUNKS + 2,)), dma((CHUNKS + 2,)), dma((CHUNKS + 2,)),
        ],
        compiler_params=pltpu.CompilerParams(
            collective_id=0, has_side_effects=True, vmem_limit_bytes=50 * 1024 * 1024),
    )(matrix, pivots, lower_inverse)


def any_kernel(R, C, nb, a_hbm, piv_hbm, linv_hbm, asw,
           a_v, piv_ref, linv_ref, sel, sel_t, pm, pf, rsbuf, tops, tp, dpart, dbuf, dh, pan, res,
           u_hi, u_lo, u_f, hit,
           load_sem, piv_sem, linv_sem, d_s, d_r, tp_s, tp_r, rs_s, rs_r, ag_s, ag_r,
           to_s, to_r, ch_s, ch_r, sb_s, sb_r):
    height, width = a_v.shape
    two = 2 * nb
    ch = two // R
    ck = height // CHUNKS
    r = lax.axis_index("row")
    c = lax.axis_index("col")
    s = lax.rem(c, 2)
    sibling = {"col": c + 1 - 2 * s}

    load = pltpu.make_async_copy(a_hbm, a_v, load_sem)
    load_piv = pltpu.make_async_copy(piv_hbm, piv_ref, piv_sem)
    load_linv = pltpu.make_async_copy(linv_hbm, linv_ref, linv_sem)
    load_piv.start()
    load.start()
    load_linv.start()

    barrier = pltpu.get_barrier_semaphore()
    for off in range(1, R):
        pl.semaphore_signal(barrier, inc=1, device_id={"row": lax.rem(r + off, R)}, device_id_type=MESH)
    has_after = c + 2 < C
    has_before = c >= 2

    @pl.when(has_after)
    def _():
        pl.semaphore_signal(barrier, inc=1, device_id={"col": jnp.minimum(c + 2, C - 1)}, device_id_type=MESH)

    @pl.when(has_before)
    def _():
        pl.semaphore_signal(barrier, inc=1, device_id={"col": jnp.maximum(c - 2, 0)}, device_id_type=MESH)

    pl.semaphore_signal(barrier, inc=1, device_id=sibling, device_id_type=MESH)

    load_piv.wait()
    shift = nb.bit_length() - 1
    rshift = R.bit_length() - 1
    lane = lax.broadcasted_iota(jnp.int32, (nb, nb), 1)
    sub = lax.broadcasted_iota(jnp.int32, (nb, nb), 0)
    for k in range(2):
        p = piv_ref[k:k + 1, :]
        block = jnp.right_shift(p, shift)
        local = jnp.left_shift(jnp.right_shift(block, rshift), shift) + jnp.bitwise_and(p, nb - 1)
        local = jnp.where(jnp.bitwise_and(block, R - 1) == r, local, -1)
        wide = jnp.broadcast_to(local, (nb, nb))
        tall = wide.astype(F32).T
        for t in range(height // nb):
            spots = slice(t * nb, (t + 1) * nb)
            sel[spots, k * nb:(k + 1) * nb] = jnp.where(wide == sub + t * nb, 1.0, 0.0).astype(BF16)
            sel_t[k * nb:(k + 1) * nb, spots] = jnp.where(
                tall == (lane + t * nb).astype(F32), 1.0, 0.0).astype(BF16)

    load.wait()
    load_linv.wait()
    pl.semaphore_wait(barrier, R + jnp.minimum(c // 2, 1) + jnp.minimum((C - 1 - c) // 2, 1))

    def remote(src, dst, send, recv, where):
        return pltpu.make_async_remote_copy(
            src_ref=src, dst_ref=dst, send_sem=send, recv_sem=recv, device_id=where, device_id_type=MESH)

    def row_peer(off):
        return {"row": lax.rem(r + off, R)}

    def tp_copy(off):
        q = jnp.minimum(r, 1)
        return remote(a_v.at[0:nb, 0:nb], tp.at[pl.ds(pl.multiple_of(q * nb, nb), nb)],
                      tp_s.at[off - 1], tp_r.at[q], row_peer(off))

    def tops_copy(off):
        q = jnp.minimum(r, 1)
        return remote(a_v.at[0:nb], tops.at[pl.ds(pl.multiple_of(q * nb, nb), nb)],
                      to_s.at[off - 1], to_r.at[q], row_peer(off))

    def d_copy(off):
        return remote(dpart, dbuf.at[off - 1], d_s.at[off - 1], d_r.at[off - 1], row_peer(off))

    def rs_copy(off):
        to = lax.rem(r + off, R)
        return remote(pm.at[pl.ds(pl.multiple_of(to * ch, ch), ch)], rsbuf.at[off - 1],
                      rs_s.at[off - 1], rs_r.at[off - 1], {"row": to})

    def ag_copy(off):
        mine = pf.at[pl.ds(pl.multiple_of(r * ch, ch), ch)]
        return remote(mine, mine, ag_s.at[off - 1], ag_r.at[off - 1], row_peer(off))

    def ag_in(off):
        src = lax.rem(r - off + R, R)
        there = pf.at[pl.ds(pl.multiple_of(src * ch, ch), ch)]
        return remote(there, there, ag_s.at[off - 1], ag_r.at[off - 1], row_peer(off))

    def piece(side, k):
        if k < CHUNKS:
            return pan.at[side, pl.ds(k * ck, ck)]
        return dh.at[side, pl.ds((k - CHUNKS) * nb, nb)]

    def chain_copy(k):
        part = piece(s, k)
        return remote(part, part, ch_s.at[k], ch_r.at[k], {"col": jnp.minimum(c + 2, C - 2 + s)})

    def sib_copy(k):
        part = piece(s, k)
        return remote(part, part, sb_s.at[k], sb_r.at[k], sibling)

    def sib_in(k):
        part = piece(1 - s, k)
        return remote(part, part, sb_s.at[k], sb_r.at[k], sibling)

    is_top = r < 2
    at_root = c < 2

    @pl.when(at_root)
    def _():
        @pl.when(is_top)
        def _():
            for off in range(1, R):
                tp_copy(off).start()
            tp[pl.ds(pl.multiple_of(jnp.minimum(r, 1) * nb, nb), nb), :] = a_v[0:nb, 0:nb]

        dpart[...] = select(sel_t[...], a_v[:, 0:nb])
        for off in range(1, R):
            d_copy(off).start()

    ones = jnp.full((two, nb), 1.0, BF16)

    @pl.loop(0, TILES)
    def _(t):
        spots = pl.ds(pl.multiple_of(t * (height // TILES), height // TILES), height // TILES)
        hit[spots, :] = mm(sel[spots, :], ones)

    def panel(first, last):
        high, middle, low = thirds(tp[...])
        for k in range(first, last):
            spots = slice(k * ck, (k + 1) * ck)
            chosen = sel[spots, :]
            placed = mm(chosen, high) + (mm(chosen, middle) + mm(chosen, low))
            pan[s, spots, :] = jnp.where(hit[spots, :] > 0.5, placed, a_v[spots, 0:nb])
            chain_copy(k).start()
            sib_copy(k).start()

    @pl.loop(0, width // nb)
    def _(t):
        spots = pl.ds(pl.multiple_of(t * nb, nb), nb)
        pm[:, spots] = select(sel_t[...], a_v[:, spots])

    @pl.when(at_root)
    def _():
        for q in range(2):
            @pl.when(r != q)
            def _():
                part = tp.at[q * nb:(q + 1) * nb]
                remote(part, part, tp_s.at[0], tp_r.at[q], row_peer(1)).wait_recv()
        panel(0, ANY_EARLY)

    for off in range(1, R):
        rs_copy(off).start()

    @pl.when(is_top)
    def _():
        for off in range(1, R):
            tops_copy(off).start()
        tops[pl.ds(pl.multiple_of(jnp.minimum(r, 1) * nb, nb), nb), :] = a_v[0:nb, :]

    @pl.when(at_root)
    def _():
        total = dpart[...]
        for off in range(1, R):
            d_copy(off).wait_recv()
            total = total + dbuf[off - 1]
        dh[s] = total
        for k in range(CHUNKS, CHUNKS + 2):
            chain_copy(k).start()
            sib_copy(k).start()
        panel(ANY_EARLY, CHUNKS)

    def forward(k):
        @pl.when(c >= 2)
        def _():
            chain_copy(k).wait_recv()

            @pl.when(c + 2 < C)
            def _():
                chain_copy(k).start()
            sib_copy(k).start()

    for k in range(ANY_EARLY):
        forward(k)
    forward(CHUNKS)
    forward(CHUNKS + 1)

    own = pl.ds(pl.multiple_of(r * ch, ch), ch)
    total = pm[own, :]
    for off in range(1, R):
        rs_copy(off).wait_recv()
        total = total + rsbuf[off - 1]
    pf[own, :] = total
    for off in range(1, R):
        ag_copy(off).start()

    left = list(range(ANY_EARLY, CHUNKS))

    def some(count):
        for _ in range(min(count, len(left))):
            forward(left.pop(0))

    sib_in(CHUNKS).wait_recv()
    sib_in(CHUNKS + 1).wait_recv()
    upper00 = jnp.where(sub <= lane, exact(linv_ref[0], dh[0, 0:nb, :]), 0.0)
    res[0] = upper_inverse(upper00, sub, lane)
    some(1)
    res[1] = exact(dh[0, nb:two, :], res[0])
    upper01 = exact(linv_ref[0], dh[1, 0:nb, :])
    rest = dh[1, nb:two, :] - exact(res[1], upper01)
    upper11 = jnp.where(sub <= lane, exact(linv_ref[1], rest), 0.0)
    res[2] = -exact(res[0], upper01)
    some(1)
    res[3] = upper_inverse(upper11, sub, lane)
    some(2)
    res[2] = exact(res[2], res[3])
    mixed = -exact(exact(linv_ref[1], res[1]), linv_ref[0])
    some(1)

    for q in range(2):
        @pl.when(r != q)
        def _():
            part = tops.at[q * nb:(q + 1) * nb]
            remote(part, part, to_s.at[0], to_r.at[q], row_peer(1)).wait_recv()

    for t in range(width // nb):
        spots = slice(t * nb, (t + 1) * nb)
        placed = select(sel[...], tops[:, spots])
        asw[:, spots] = jnp.where(hit[...] > 0.5, placed, a_v[:, spots])
        some(1)

    for off in range(1, R):
        ag_in(off).wait_recv()

    inv_low0 = linv_ref[0]
    inv_low1 = linv_ref[1]
    u_f[0:nb, :] = dot3(halves(inv_low0), halves(pf[0:nb, :]))
    u_f[nb:two, :] = (dot3(halves(mixed), halves(pf[0:nb, :]))
                      + dot3(halves(inv_low1), halves(pf[nb:two, :])))
    high, low = halves(u_f[...])
    u_hi[...] = high
    u_lo[...] = low

    step = height // TILES
    inv0 = halves(res[0])
    cross = halves(res[2])
    inv1 = halves(res[3])

    def update(t, start):
        spots = pl.ds(start, step)
        left0 = halves(pan[0, spots, :])
        left1 = halves(pan[1, spots, :])
        low0 = dot3(left0, inv0)
        low1 = dot3(left0, cross) + dot3(left1, inv1)
        high, low = halves(jnp.concatenate([low0, low1], axis=1))
        asw[spots, :] = asw[spots, :] - dot3((high, low), (u_hi[...], u_lo[...]))

        @pl.when(c == 0)
        def _():
            asw[spots, 0:nb] = low0

        @pl.when(c == 1)
        def _():
            asw[spots, 0:nb] = low1

    per_tile = CHUNKS // TILES
    for t in range(TILES):
        some(1)
        while left and left[0] < (t + 1) * per_tile:
            some(1)
        for k in range(t * per_tile, (t + 1) * per_tile):
            sib_in(k).wait_recv()
        update(t, t * step)
        if t == 0:
            @pl.when(r == 0)
            def _():
                asw[0:nb, :] = u_f[0:nb, :]

                @pl.when(c == 0)
                def _():
                    asw[0:nb, 0:nb] = jnp.where(sub <= lane, u_f[0:nb, 0:nb], 0.0)

            @pl.when(r == 1)
            def _():
                asw[0:nb, :] = u_f[nb:two, :]

                @pl.when(c == 0)
                def _():
                    asw[0:nb, 0:nb] = res[1]

                @pl.when(c == 1)
                def _():
                    asw[0:nb, 0:nb] = jnp.where(sub <= lane, u_f[nb:two, 0:nb], 0.0)

    for off in range(1, R):
        rs_copy(off).wait_send()
        ag_copy(off).wait_send()

    @pl.when(is_top)
    def _():
        for off in range(1, R):
            tops_copy(off).wait_send()

        @pl.when(at_root)
        def _():
            for off in range(1, R):
                tp_copy(off).wait_send()

    for k in range(CHUNKS + 2):
        sib_copy(k).wait_send()

        @pl.when(c + 2 < C)
        def _():
            chain_copy(k).wait_send()

    @pl.when(at_root)
    def _():
        for off in range(1, R):
            d_copy(off).wait_send()


def any_device(matrix, pivots, lower_inverse):
    R = lax.axis_size("row")
    C = lax.axis_size("col")
    height, width = matrix.shape
    nb = lower_inverse.shape[1]
    two = 2 * nb
    dma = pltpu.SemaphoreType.DMA
    vm = pltpu.VMEM
    return pl.pallas_call(
        functools.partial(any_kernel, R, C, nb),
        out_shape=jax.ShapeDtypeStruct((height, width), F32),
        in_specs=[pl.BlockSpec(memory_space=pl.ANY)] * 3,
        out_specs=pl.BlockSpec(memory_space=pltpu.VMEM),
        scratch_shapes=[
            vm((height, width), F32), vm((2, nb), jnp.int32), vm((2, nb, nb), F32),
            vm((height, two), BF16), vm((two, height), BF16),
            vm((two, width), F32), vm((two, width), F32),
            vm((R - 1, two // R, width), F32), vm((two, width), F32),
            vm((two, nb), F32), vm((two, nb), F32), vm((R - 1, two, nb), F32),
            vm((2, two, nb), F32), vm((2, height, nb), F32), vm((4, nb, nb), F32),
            vm((two, width), BF16), vm((two, width), BF16), vm((two, width), F32),
            vm((height, nb), F32),
            dma, dma, dma, dma((R - 1,)), dma((R - 1,)), dma((R - 1,)), dma((2,)),
            dma((R - 1,)), dma((R - 1,)), dma((R - 1,)), dma((R - 1,)),
            dma((R - 1,)), dma((2,)), dma((CHUNKS + 2,)), dma((CHUNKS + 2,)),
            dma((CHUNKS + 2,)), dma((CHUNKS + 2,)),
        ],
        compiler_params=pltpu.CompilerParams(
            collective_id=1, has_side_effects=True, vmem_limit_bytes=50 * 1024 * 1024),
    )(matrix, pivots, lower_inverse)


def most_kernel(R, nb, piv_ref, out_ref):
    owner = jnp.bitwise_and(jnp.right_shift(piv_ref[...], nb.bit_length() - 1), R - 1)
    most = jnp.zeros((2, 1), F32)
    for q in range(R):
        most = jnp.maximum(most, jnp.sum(jnp.where(owner == q, 1.0, 0.0), axis=1, keepdims=True))
    out_ref[0] = jnp.max(most).astype(jnp.int32)


def on_device(matrix, pivots, lower_inverse):
    R = lax.axis_size("row")
    nb = lower_inverse.shape[1]
    most = pl.pallas_call(
        functools.partial(most_kernel, R, nb),
        out_shape=jax.ShapeDtypeStruct((1,), jnp.int32),
        in_specs=[pl.BlockSpec(memory_space=pltpu.VMEM)],
        out_specs=pl.BlockSpec(memory_space=pltpu.SMEM),
    )(pivots)
    return lax.cond(most[0] <= room(R, nb), even_device, any_device, matrix, pivots, lower_inverse)


def solution(mesh):
    return jax.shard_map(
        on_device,
        mesh=mesh,
        in_specs=(P("row", "col"), P(), P()),
        out_specs=P("row", "col"),
        check_vma=False,
    )
```

```python
import functools

import jax
import jax.numpy as jnp
from jax import lax
from jax.experimental import pallas as pl
from jax.experimental.pallas import tpu as pltpu
from jax.sharding import PartitionSpec as P

MESH = pl.DeviceIdType.MESH
F32 = jnp.float32
BF16 = jnp.bfloat16
CHUNKS = 16
EARLY = 1
MIDDLE = 12
ANY_EARLY = 3
FAR = 4
INNER = (1, 2, 2, 2)
LAST = (1, 1, 0, 2)
PASS = 0
LATE_TILE = 3
BRING = 1
TILES = 4


def mm(left, right):
    return jnp.dot(left, right, preferred_element_type=F32)


def exact(left, right):
    return jnp.dot(left, right, precision=lax.Precision.HIGHEST, preferred_element_type=F32)


def halves(value):
    high = value.astype(BF16)
    return high, (value - high.astype(F32)).astype(BF16)


def thirds(value):
    high = value.astype(BF16)
    rest = value - high.astype(F32)
    middle = rest.astype(BF16)
    return high, middle, (rest - middle.astype(F32)).astype(BF16)


def select(chosen, value):
    high, middle, low = thirds(value)
    return mm(chosen, high) + (mm(chosen, middle) + mm(chosen, low))


def dot3(left, right):
    left_high, left_low = left
    right_high, right_low = right
    return mm(left_high, right_high) + (mm(left_low, right_high) + mm(left_high, right_low))


def upper_inverse(upper, rows, cols):
    on_diag = rows == cols
    eye = jnp.where(on_diag, 1.0, 0.0)
    kept = jnp.where(on_diag, upper, 0.0)
    scaled = upper / jnp.sum(kept, axis=1, keepdims=True)
    power = jnp.where(rows < cols, -scaled, 0.0)
    result = eye + power
    reach = 2
    while reach < upper.shape[0]:
        power = exact(power, power)
        result = result + exact(result, power)
        reach = reach * 2
    return result / jnp.sum(kept, axis=0, keepdims=True)


def select2(chosen, value):
    high, low = halves(value)
    return mm(chosen, high) + mm(chosen, low)


def close(left, right):
    left_high, left_low = halves(left)
    right_high, right_low = halves(right)
    return mm(jnp.concatenate([left_high, left_low, left_high], axis=1),
              jnp.concatenate([right_high, right_high, right_low], axis=0))


def quick_inverse(upper, rows, cols, between):
    on_diag = rows == cols
    eye = jnp.where(on_diag, 1.0, 0.0)
    kept = jnp.where(on_diag, upper, 0.0)
    scaled = upper / jnp.sum(kept, axis=1, keepdims=True)
    power = jnp.where(rows < cols, -scaled, 0.0)
    result = eye + power
    reach = 2
    while reach < upper.shape[0]:
        power = close(power, power)
        result = result + close(result, power)
        reach = reach * 2
        if reach in (8, 32):
            between(1)
    return result / jnp.sum(kept, axis=0, keepdims=True)


def room(R, nb):
    return (nb // R + 31) // 16 * 16


def kernel(R, C, nb, a_hbm, piv_ref, linv_ref, asw,
           sel, sel_t, place, split, tcomp, pall, dall, tops, tpan, dh, pan, res, inv3, me3, w3, tw, u_f, hit,
           load_sem, tq_s, tq_r, da_s, da_r, to_s, to_r,
           ag_s, ag_r, ch_s, ch_r, sb_s, sb_r):
    height, width = asw.shape
    two = 2 * nb
    cap = room(R, nb)
    W = 2 * cap
    ck = height // CHUNKS
    NJ = width // nb
    r = lax.axis_index("row")
    c = lax.axis_index("col")
    s = lax.rem(c, 2)
    sibling = {"col": c + 1 - 2 * s}
    top_half = jnp.minimum(r, 1)
    odd = lax.rem(r, 2)
    relay = R == 4

    def flip(bit):
        if bit == 1:
            return r + 1 - 2 * odd
        if bit == 2:
            return lax.rem(r + 2, 4)
        return 3 - r

    def cols(j):
        return pl.ds(j * nb, nb)

    def load(j):
        return pltpu.make_async_copy(a_hbm.at[:, cols(j)], asw.at[:, cols(j)], load_sem.at[j])

    for j in range(NJ):
        load(j).start()

    has_after = c + 2 < C
    has_before = c >= 2
    at_root = c < 2
    is_top = r < 2

    barrier = pltpu.get_barrier_semaphore()
    for off in range(1, R):
        pl.semaphore_signal(barrier, inc=1, device_id={"row": lax.rem(r + off, R)}, device_id_type=MESH)

    @pl.when(has_after)
    def _():
        pl.semaphore_signal(barrier, inc=1, device_id={"col": jnp.minimum(c + 2, C - 1)}, device_id_type=MESH)

    @pl.when(has_before)
    def _():
        pl.semaphore_signal(barrier, inc=1, device_id={"col": jnp.maximum(c - 2, 0)}, device_id_type=MESH)

    pl.semaphore_signal(barrier, inc=1, device_id=sibling, device_id_type=MESH)

    pl.semaphore_wait(barrier, R + jnp.minimum(c // 2, 1) + jnp.minimum((C - 1 - c) // 2, 1))

    def remote(src, dst, send, recv, where):
        return pltpu.make_async_remote_copy(
            src_ref=src, dst_ref=dst, send_sem=send, recv_sem=recv, device_id=where, device_id_type=MESH)

    def rows(index, count):
        return pl.ds(pl.multiple_of(index * count, count), count)

    def peer(off):
        return lax.rem(r + off, R)

    def origin(off):
        return lax.rem(r - off + R, R)

    def da_copy(off):
        part = dall.at[s, rows(r, W)]
        return remote(part, part, da_s.at[off - 1], da_r.at[off - 1], {"row": peer(off)})

    def da_in(off):
        part = dall.at[s, rows(origin(off), W)]
        return remote(part, part, da_s.at[off - 1], da_r.at[off - 1], {"row": peer(off)})

    def tq_copy(off):
        return remote(tcomp.at[0, rows(peer(off), cap)], tpan.at[s, rows(top_half, cap)],
                      tq_s.at[off - 1], tq_r.at[top_half], {"row": peer(off)})

    def tz_copy(off):
        return remote(tcomp.at[0, rows(peer(off), cap)], tops.at[0, rows(top_half, cap)],
                      tq_s.at[off - 1], tq_r.at[top_half], {"row": peer(off)})

    def to_copy(off):
        return remote(tcomp.at[pl.ds(1, NJ - 1), rows(peer(off), cap)],
                      tops.at[pl.ds(1, NJ - 1), rows(top_half, cap)],
                      to_s.at[off - 1], to_r.at[top_half], {"row": peer(off)})

    def tq_in(half):
        part = tpan.at[s, pl.ds(half * cap, cap)]
        return remote(part, part, tq_s.at[0], tq_r.at[half], {"row": peer(1)})

    def tz_in(half):
        part = tops.at[0, pl.ds(half * cap, cap)]
        return remote(part, part, tq_s.at[0], tq_r.at[half], {"row": peer(1)})

    def to_in(half):
        part = tops.at[pl.ds(1, NJ - 1), pl.ds(half * cap, cap)]
        return remote(part, part, to_s.at[0], to_r.at[half], {"row": peer(1)})

    def from_tops(copy):
        for half in range(2):
            @pl.when(r != half)
            def _():
                copy(half).wait_recv()

    def ag_copy(j, i):
        at = j * (R - 1) + i
        if not relay:
            part = pall.at[j, rows(r, W)]
            return remote(part, part, ag_s.at[at], ag_r.at[at], {"row": peer(i + 1)})
        if i < 2:
            part = pall.at[j, rows(r, W)]
            return remote(part, part, ag_s.at[at], ag_r.at[at], {"row": flip(i + 1)})
        bit = 1 + j % 2
        part = pall.at[j, rows(flip(3 - bit), W)]
        return remote(part, part, ag_s.at[at], ag_r.at[at], {"row": flip(bit)})

    def ag_in(j, i):
        at = j * (R - 1) + i
        src = flip(i + 1) if relay else origin(i + 1)
        part = pall.at[j, rows(src, W)]
        return remote(part, part, ag_s.at[at], ag_r.at[at], {"row": peer(1)})

    def ag_start(j):
        for i in range(2 if relay else R - 1):
            ag_copy(j, i).start()

    def ag_relay_from(j):
        return 1 - j % 2

    def past_root(j, go):
        if j == 0:
            pl.when(has_before)(go)
        else:
            go()

    def ag_pass(j):
        if relay:
            def go():
                ag_in(j, ag_relay_from(j)).wait_recv()
                ag_copy(j, 2).start()
            past_root(j, go)

    def ag_finish(j):
        def go():
            for i in range(R - 1):
                if not (relay and i == ag_relay_from(j)):
                    ag_in(j, i).wait_recv()
        past_root(j, go)

    TQ, DQ = CHUNKS, CHUNKS + 1

    def piece(k):
        if k < CHUNKS:
            return pan.at[s, pl.ds(k * ck, ck)]
        if k == TQ:
            return tpan.at[s, pl.ds(0, W)]
        return dall.at[s, rows(r, W)]

    after = {"col": jnp.minimum(c + 2, C - 2 + s)}

    def chain_copy(k):
        return remote(piece(k), piece(k), ch_s.at[k], ch_r.at[k], after)

    def root_copy(k):
        return remote(a_hbm.at[pl.ds(k * ck, ck), cols(0)], piece(k), ch_s.at[k], ch_r.at[k], after)

    def spread(k, side):
        if k < CHUNKS:
            return pan.at[side, pl.ds(k * ck, ck)]
        return tpan.at[side, pl.ds(0, W)] if k == TQ else dall.at[side]

    def sib_copy(k):
        return remote(spread(k, s), spread(k, s), sb_s.at[k], sb_r.at[k], sibling)

    def root_sib(k):
        return remote(a_hbm.at[pl.ds(k * ck, ck), cols(0)], spread(k, s), sb_s.at[k], sb_r.at[k], sibling)

    def sib_in(k):
        return remote(spread(k, 1 - s), spread(k, 1 - s), sb_s.at[k], sb_r.at[k], sibling)

    def forward(k, inner):
        @pl.when(has_before & (has_after if inner else c + 2 >= C))
        def _():
            chain_copy(k).wait_recv()
            if inner:
                chain_copy(k).start()
            if k == DQ:
                for off in range(1, R):
                    da_copy(off).start()
            else:
                sib_copy(k).start()

    order = list(range(EARLY)) + [DQ] + list(range(EARLY, MIDDLE)) + [TQ] + list(range(MIDDLE, CHUNKS))
    left = order[:]
    late = order[:]

    def step_on(queue, count):
        for _ in range(min(count, len(queue))):
            forward(queue.pop(0), queue is left)

    def some(count):
        step_on(left, count)
        step_on(late, count)

    def until(k):
        for queue in (left, late):
            while k in queue:
                step_on(queue, 1)

    def from_root(first, last):
        for k in range(first, last):
            @pl.when(has_after)
            def _():
                root_copy(k).start()
            root_sib(k).start()

    @pl.when(at_root)
    def _():
        from_root(0, EARLY)

    shift = nb.bit_length() - 1
    rshift = R.bit_length() - 1
    lane = lax.broadcasted_iota(jnp.int32, (nb, nb), 1)
    sub = lax.broadcasted_iota(jnp.int32, (nb, nb), 0)
    lane_f = lane.astype(F32)
    sub_f = sub.astype(F32)
    before = jnp.where(sub < lane, 1.0, 0.0).astype(BF16)
    owners, slots, talls = [], [], []
    for k in range(2):
        p = piv_ref[k:k + 1, :]
        block = jnp.right_shift(p, shift)
        owner = jnp.bitwise_and(block, R - 1)
        local = jnp.left_shift(jnp.right_shift(block, rshift), shift) + jnp.bitwise_and(p, nb - 1)
        hot = jnp.where(jnp.broadcast_to(owner, (16, nb)) == sub[0:16], 1.0, 0.0)
        rank = mm(hot.astype(BF16), before)
        slot = jnp.sum(hot * rank, axis=0, keepdims=True)
        mine = jnp.where(owner == r, slot, -1.0)
        match = jnp.broadcast_to(mine, (cap, nb)) == sub_f[0:cap]
        value = jnp.broadcast_to(local.astype(F32) + 1.0, (cap, nb))
        spot = jnp.sum(jnp.where(match, value, 0.0), axis=1, keepdims=True) - 1.0
        owners.append(owner)
        slots.append(slot)
        talls.append(jnp.broadcast_to(spot, (cap, nb)))
    if W < nb:
        talls.append(jnp.full((nb - W, nb), -1.0, F32))
    tall = jnp.concatenate(talls, axis=0)
    for t in range(height // nb):
        spots = slice(t * nb, (t + 1) * nb)
        sel_t[:, spots] = jnp.where(tall[0:W] == lane_f[0:W] + float(t * nb), 1.0, 0.0).astype(BF16)

    load(0).wait()
    first = select(sel_t[...], asw[:, 0:nb])

    @pl.when(at_root)
    def _():
        dall[s, rows(r, W), :] = first

        @pl.when(has_after)
        def _():
            chain_copy(DQ).start()
        for off in range(1, R):
            da_copy(off).start()
        from_root(EARLY, MIDDLE)
        pan[s] = asw[:, 0:nb]

    @pl.when(has_before)
    def _():
        pall[0, rows(r, W), :] = first
        ag_start(0)

    def collect(start, stop):
        value = select2(sel_t[...], asw[:, start * nb:stop * nb])
        for j in range(start, stop):
            pall[j, rows(r, W), :] = value[:, (j - start) * nb:(j - start + 1) * nb]

    load(1).wait()
    collect(1, 2)
    for j in range(2, NJ):
        load(j).wait()
    for j in range(2, NJ, 2):
        collect(j, min(j + 2, NJ))

    @pl.when(c >= FAR)
    def _():
        for j in range(1, NJ):
            ag_start(j)

    if W < nb:
        for j in range(NJ):
            tops[j, W:nb, :] = jnp.zeros((nb - W, nb), F32)
        for k in range(2):
            tpan[k, W:nb, :] = jnp.zeros((nb - W, nb), F32)
    wide = tall.T
    for t in range(height // nb):
        spots = slice(t * nb, (t + 1) * nb)
        value = jnp.where(wide == sub_f + float(t * nb), 1.0, 0.0).astype(BF16)
        sel[spots, 0:nb] = value
        sel[spots, nb:two] = value
    for k in range(2):
        aim = owners[k].astype(F32) * float(W) + (slots[k] + float(k * cap))
        aim = jnp.broadcast_to(aim, (nb, nb)).T
        for t in range(R * W // nb):
            place[k * nb:(k + 1) * nb, t * nb:(t + 1) * nb] = jnp.where(
                aim == lane_f + float(t * nb), 1.0, 0.0).astype(BF16)

    until(DQ)

    @pl.when(c < FAR)
    def _():
        for j in range(1, NJ):
            ag_start(j)

    @pl.when(is_top)
    def _():
        owner = jnp.where(r == 0, owners[0], owners[1])
        slot = jnp.where(r == 0, slots[0], slots[1])
        for q in range(R):
            aim = jnp.where(owner == q, slot, -1.0)
            aim = jnp.where(jnp.broadcast_to(aim, (cap, nb)) == sub_f[0:cap], 1.0, 0.0).astype(BF16)
            split[q * cap:(q + 1) * cap, 0:nb] = aim
            split[q * cap:(q + 1) * cap, nb:two] = aim
        value = mm(split[...], jnp.concatenate(halves(asw[0:nb, :]), axis=0))
        for j in range(NJ):
            tcomp[j] = value[:, j * nb:(j + 1) * nb]
        own = jnp.where(r == 0, value[0:cap, :], value[cap:2 * cap, :])

        @pl.when(at_root)
        def _():
            tpan[s, rows(top_half, cap), :] = own[:, 0:nb]
            for off in range(1, R):
                tq_copy(off).start()

        @pl.when(has_before)
        def _():
            tops[0, rows(top_half, cap), :] = own[:, 0:nb]
            for off in range(1, R):
                tz_copy(off).start()

        for off in range(1, R):
            to_copy(off).start()
        for j in range(1, NJ):
            tops[j, rows(top_half, cap), :] = own[:, j * nb:(j + 1) * nb]

    step_on(left, INNER[0])
    step_on(late, LAST[0])
    ones = jnp.full((two, nb), 1.0, BF16)

    @pl.loop(0, TILES)
    def _(t):
        spots = rows(t, height // TILES)
        hit[spots, :] = mm(sel[spots, :], ones)

    step_on(left, INNER[1])
    step_on(late, LAST[1])
    ag_pass(0)
    step_on(left, INNER[2])
    step_on(late, LAST[2])
    for off in range(1, R):
        da_in(off).wait_recv()
    sib_copy(DQ).start()

    @pl.when(at_root)
    def _():
        from_tops(tq_in)

        @pl.when(has_after)
        def _():
            chain_copy(TQ).start()
        sib_copy(TQ).start()
        from_root(MIDDLE, CHUNKS)
        tops[0] = tpan[s]
        pall[0] = dall[s]

    step_on(left, INNER[3])
    step_on(late, LAST[3])
    sib_in(DQ).wait_recv()
    both = select(place[...], jnp.concatenate([dall[0], dall[1]], axis=1))
    dh[0] = both[:, 0:nb]
    dh[1] = both[:, nb:two]
    upper00 = jnp.where(sub <= lane, close(linv_ref[0], dh[0, 0:nb, :]), 0.0)
    upper01 = close(linv_ref[0], dh[1, 0:nb, :])
    some(1)
    ag_pass(1)
    ag_pass(2)
    res[0] = quick_inverse(upper00, sub, lane, some)
    some(1)
    ag_pass(3)
    res[1] = close(dh[0, nb:two, :], res[0])
    rest = dh[1, nb:two, :] - close(res[1], upper01)
    upper11 = jnp.where(sub <= lane, close(linv_ref[1], rest), 0.0)
    res[2] = -close(res[0], upper01)
    mixed = -close(close(linv_ref[1], res[1]), linv_ref[0])
    blank = jnp.zeros((nb, nb), F32)
    high, low = halves(jnp.concatenate([
        jnp.concatenate([linv_ref[0], blank], axis=1),
        jnp.concatenate([mixed, linv_ref[1]], axis=1)], axis=0))
    span = R * W
    high = mm(high, place[...]).astype(BF16)
    me3[:, 0:span] = high
    me3[:, span:2 * span] = mm(low, place[...]).astype(BF16)
    me3[:, 2 * span:3 * span] = high
    some(1)
    res[3] = quick_inverse(upper11, sub, lane, some)
    for j in range(4 if PASS == 0 else 3, NJ):
        ag_pass(j)
    some(1)

    def stack(value):
        high, low = halves(value)
        return jnp.concatenate([high, high, low], axis=0)

    def row_stack(value):
        high, low = halves(value)
        return jnp.concatenate([high, low, high], axis=1)

    inverse = jnp.concatenate([
        jnp.concatenate([res[0], close(res[2], res[3])], axis=1),
        jnp.concatenate([blank, res[3]], axis=1)], axis=0)
    inv3[...] = stack(inverse)
    left3 = row_stack(inverse)
    for j in range(0, NJ, 2):
        ag_finish(j)
        ag_finish(j + 1)
        spots = slice(j * nb, (j + 2) * nb)
        value = mm(me3[...], stack(jnp.concatenate([pall[j], pall[j + 1]], axis=1)))
        u_f[:, spots] = value
        w3[:, spots] = stack(mm(left3, stack(value)))
        some(1)

    def update(start, count):
        spots = slice(start, start + count)
        here = hit[spots, :] > 0.5
        kept = row_stack(jnp.concatenate([
            jnp.where(here, 0.0, pan[0, spots, :]), jnp.where(here, 0.0, pan[1, spots, :])], axis=1))
        asw[spots, :] = asw[spots, :] - mm(kept, w3[...])

        @pl.when(at_root)
        def _():
            value = mm(kept, inv3[...])
            value = jnp.where(c == 0, value[:, 0:nb], value[:, nb:two])
            asw[spots, 0:nb] = jnp.where(here, asw[spots, 0:nb], value)

    def bring():
        until(TQ)
        sib_in(TQ).wait_recv()
        from_tops(to_in)

        @pl.when(has_before)
        def _():
            from_tops(tz_in)

        tp = row_stack(jnp.concatenate([tpan[0], tpan[1]], axis=1))
        moved = jnp.concatenate([tops[j] for j in range(NJ)], axis=1) - mm(tp, w3[...])
        tw[0:nb, :], tw[nb:two, :] = halves(moved)

        @pl.when(at_root)
        def _():
            value = mm(tp, inv3[...])
            tw[0:nb, 0:nb], tw[nb:two, 0:nb] = halves(jnp.where(c == 0, value[:, 0:nb], value[:, nb:two]))

        for t in range(TILES):
            spots = slice(t * step, (t + 1) * step)
            here = hit[spots, :] > 0.5
            moved = mm(sel[spots, :], tw[...])
            for j in range(NJ):
                part = slice(j * nb, (j + 1) * nb)
                asw[spots, part] = jnp.where(here, moved[:, part], asw[spots, part])
            some(BRING)

    def finish_top():
        @pl.when(r == 0)
        def _():
            asw[0:nb, :] = u_f[0:nb, :]

            @pl.when(c == 0)
            def _():
                asw[0:nb, 0:nb] = jnp.where(sub <= lane, u_f[0:nb, 0:nb], 0.0)

        @pl.when(r == 1)
        def _():
            asw[0:nb, :] = u_f[nb:two, :]

            @pl.when(c == 0)
            def _():
                asw[0:nb, 0:nb] = res[1]

            @pl.when(c == 1)
            def _():
                asw[0:nb, 0:nb] = jnp.where(sub <= lane, u_f[nb:two, 0:nb], 0.0)

    step = height // TILES
    tiles = [(t * step, step) for t in range(TILES - 1)]
    tiles += [(height - step, step // 2), (height - step // 2, step // 2)]
    for at, (start, count) in enumerate(tiles):
        if at == LATE_TILE:
            bring()
            finish_top()
        for queue in (left, late):
            while any(k < CHUNKS and k * ck < start + count for k in queue):
                step_on(queue, 1)
        for k in range(start // ck, (start + count) // ck):
            sib_in(k).wait_recv()
        update(start, count)
        some(1)

    for j in range(NJ):
        def gone(j=j):
            for i in range(R - 1):
                ag_copy(j, i).wait_send()
        past_root(j, gone)

    @pl.when(is_top)
    def _():
        for off in range(1, R):
            to_copy(off).wait_send()
            tq_copy(off).wait_send()

    for off in range(1, R):
        da_copy(off).wait_send()

    for k in range(CHUNKS + 2):
        sib_copy(k).wait_send()

        @pl.when(has_after)
        def _():
            chain_copy(k).wait_send()


def even_device(matrix, pivots, lower_inverse):
    R = lax.axis_size("row")
    C = lax.axis_size("col")
    height, width = matrix.shape
    nb = lower_inverse.shape[1]
    two = 2 * nb
    nj = width // nb
    cap = room(R, nb)
    dma = pltpu.SemaphoreType.DMA
    vm = pltpu.VMEM
    return pl.pallas_call(
        functools.partial(kernel, R, C, nb),
        out_shape=jax.ShapeDtypeStruct((height, width), F32),
        in_specs=[pl.BlockSpec(memory_space=pl.ANY)] + [pl.BlockSpec(memory_space=pltpu.VMEM)] * 2,
        out_specs=pl.BlockSpec(memory_space=pltpu.VMEM),
        scratch_shapes=[
            vm((height, two), BF16), vm((2 * cap, height), BF16), vm((two, 2 * cap * R), BF16),
            vm((cap * R, two), BF16), vm((nj, cap * R, nb), F32), vm((nj, 2 * cap * R, nb), F32),
            vm((2, 2 * cap * R, nb), F32), vm((nj, nb, nb), F32), vm((2, nb, nb), F32),
            vm((2, two, nb), F32), vm((2, height, nb), F32), vm((4, nb, nb), F32),
            vm((3 * two, two), BF16), vm((two, 6 * cap * R), BF16),
            vm((3 * two, width), BF16), vm((two, width), BF16), vm((two, width), F32),
            vm((height, nb), F32),
            dma((nj,)), dma((R - 1,)), dma((2,)), dma((R - 1,)), dma((R - 1,)),
            dma((R - 1,)), dma((2,)),
            dma((nj * (R - 1),)), dma((nj * (R - 1),)),
            dma((CHUNKS + 2,)), dma((CHUNKS + 2,)), dma((CHUNKS + 2,)), dma((CHUNKS + 2,)),
        ],
        compiler_params=pltpu.CompilerParams(
            collective_id=0, has_side_effects=True, vmem_limit_bytes=50 * 1024 * 1024),
    )(matrix, pivots, lower_inverse)


def any_kernel(R, C, nb, a_hbm, piv_hbm, linv_hbm, asw,
           a_v, piv_ref, linv_ref, sel, sel_t, pm, pf, rsbuf, tops, tp, dpart, dbuf, dh, pan, res,
           u_hi, u_lo, u_f, hit,
           load_sem, piv_sem, linv_sem, d_s, d_r, tp_s, tp_r, rs_s, rs_r, ag_s, ag_r,
           to_s, to_r, ch_s, ch_r, sb_s, sb_r):
    height, width = a_v.shape
    two = 2 * nb
    ch = two // R
    ck = height // CHUNKS
    r = lax.axis_index("row")
    c = lax.axis_index("col")
    s = lax.rem(c, 2)
    sibling = {"col": c + 1 - 2 * s}

    load = pltpu.make_async_copy(a_hbm, a_v, load_sem)
    load_piv = pltpu.make_async_copy(piv_hbm, piv_ref, piv_sem)
    load_linv = pltpu.make_async_copy(linv_hbm, linv_ref, linv_sem)
    load_piv.start()
    load.start()
    load_linv.start()

    barrier = pltpu.get_barrier_semaphore()
    for off in range(1, R):
        pl.semaphore_signal(barrier, inc=1, device_id={"row": lax.rem(r + off, R)}, device_id_type=MESH)
    has_after = c + 2 < C
    has_before = c >= 2

    @pl.when(has_after)
    def _():
        pl.semaphore_signal(barrier, inc=1, device_id={"col": jnp.minimum(c + 2, C - 1)}, device_id_type=MESH)

    @pl.when(has_before)
    def _():
        pl.semaphore_signal(barrier, inc=1, device_id={"col": jnp.maximum(c - 2, 0)}, device_id_type=MESH)

    pl.semaphore_signal(barrier, inc=1, device_id=sibling, device_id_type=MESH)

    load_piv.wait()
    shift = nb.bit_length() - 1
    rshift = R.bit_length() - 1
    lane = lax.broadcasted_iota(jnp.int32, (nb, nb), 1)
    sub = lax.broadcasted_iota(jnp.int32, (nb, nb), 0)
    for k in range(2):
        p = piv_ref[k:k + 1, :]
        block = jnp.right_shift(p, shift)
        local = jnp.left_shift(jnp.right_shift(block, rshift), shift) + jnp.bitwise_and(p, nb - 1)
        local = jnp.where(jnp.bitwise_and(block, R - 1) == r, local, -1)
        wide = jnp.broadcast_to(local, (nb, nb))
        tall = wide.astype(F32).T
        for t in range(height // nb):
            spots = slice(t * nb, (t + 1) * nb)
            sel[spots, k * nb:(k + 1) * nb] = jnp.where(wide == sub + t * nb, 1.0, 0.0).astype(BF16)
            sel_t[k * nb:(k + 1) * nb, spots] = jnp.where(
                tall == (lane + t * nb).astype(F32), 1.0, 0.0).astype(BF16)

    load.wait()
    load_linv.wait()
    pl.semaphore_wait(barrier, R + jnp.minimum(c // 2, 1) + jnp.minimum((C - 1 - c) // 2, 1))

    def remote(src, dst, send, recv, where):
        return pltpu.make_async_remote_copy(
            src_ref=src, dst_ref=dst, send_sem=send, recv_sem=recv, device_id=where, device_id_type=MESH)

    def row_peer(off):
        return {"row": lax.rem(r + off, R)}

    def tp_copy(off):
        q = jnp.minimum(r, 1)
        return remote(a_v.at[0:nb, 0:nb], tp.at[pl.ds(pl.multiple_of(q * nb, nb), nb)],
                      tp_s.at[off - 1], tp_r.at[q], row_peer(off))

    def tops_copy(off):
        q = jnp.minimum(r, 1)
        return remote(a_v.at[0:nb], tops.at[pl.ds(pl.multiple_of(q * nb, nb), nb)],
                      to_s.at[off - 1], to_r.at[q], row_peer(off))

    def d_copy(off):
        return remote(dpart, dbuf.at[off - 1], d_s.at[off - 1], d_r.at[off - 1], row_peer(off))

    def rs_copy(off):
        to = lax.rem(r + off, R)
        return remote(pm.at[pl.ds(pl.multiple_of(to * ch, ch), ch)], rsbuf.at[off - 1],
                      rs_s.at[off - 1], rs_r.at[off - 1], {"row": to})

    def ag_copy(off):
        mine = pf.at[pl.ds(pl.multiple_of(r * ch, ch), ch)]
        return remote(mine, mine, ag_s.at[off - 1], ag_r.at[off - 1], row_peer(off))

    def ag_in(off):
        src = lax.rem(r - off + R, R)
        there = pf.at[pl.ds(pl.multiple_of(src * ch, ch), ch)]
        return remote(there, there, ag_s.at[off - 1], ag_r.at[off - 1], row_peer(off))

    def piece(side, k):
        if k < CHUNKS:
            return pan.at[side, pl.ds(k * ck, ck)]
        return dh.at[side, pl.ds((k - CHUNKS) * nb, nb)]

    def chain_copy(k):
        part = piece(s, k)
        return remote(part, part, ch_s.at[k], ch_r.at[k], {"col": jnp.minimum(c + 2, C - 2 + s)})

    def sib_copy(k):
        part = piece(s, k)
        return remote(part, part, sb_s.at[k], sb_r.at[k], sibling)

    def sib_in(k):
        part = piece(1 - s, k)
        return remote(part, part, sb_s.at[k], sb_r.at[k], sibling)

    is_top = r < 2
    at_root = c < 2

    @pl.when(at_root)
    def _():
        @pl.when(is_top)
        def _():
            for off in range(1, R):
                tp_copy(off).start()
            tp[pl.ds(pl.multiple_of(jnp.minimum(r, 1) * nb, nb), nb), :] = a_v[0:nb, 0:nb]

        dpart[...] = select(sel_t[...], a_v[:, 0:nb])
        for off in range(1, R):
            d_copy(off).start()

    ones = jnp.full((two, nb), 1.0, BF16)

    @pl.loop(0, TILES)
    def _(t):
        spots = pl.ds(pl.multiple_of(t * (height // TILES), height // TILES), height // TILES)
        hit[spots, :] = mm(sel[spots, :], ones)

    def panel(first, last):
        high, middle, low = thirds(tp[...])
        for k in range(first, last):
            spots = slice(k * ck, (k + 1) * ck)
            chosen = sel[spots, :]
            placed = mm(chosen, high) + (mm(chosen, middle) + mm(chosen, low))
            pan[s, spots, :] = jnp.where(hit[spots, :] > 0.5, placed, a_v[spots, 0:nb])
            chain_copy(k).start()
            sib_copy(k).start()

    @pl.loop(0, width // nb)
    def _(t):
        spots = pl.ds(pl.multiple_of(t * nb, nb), nb)
        pm[:, spots] = select(sel_t[...], a_v[:, spots])

    @pl.when(at_root)
    def _():
        for q in range(2):
            @pl.when(r != q)
            def _():
                part = tp.at[q * nb:(q + 1) * nb]
                remote(part, part, tp_s.at[0], tp_r.at[q], row_peer(1)).wait_recv()
        panel(0, ANY_EARLY)

    for off in range(1, R):
        rs_copy(off).start()

    @pl.when(is_top)
    def _():
        for off in range(1, R):
            tops_copy(off).start()
        tops[pl.ds(pl.multiple_of(jnp.minimum(r, 1) * nb, nb), nb), :] = a_v[0:nb, :]

    @pl.when(at_root)
    def _():
        total = dpart[...]
        for off in range(1, R):
            d_copy(off).wait_recv()
            total = total + dbuf[off - 1]
        dh[s] = total
        for k in range(CHUNKS, CHUNKS + 2):
            chain_copy(k).start()
            sib_copy(k).start()
        panel(ANY_EARLY, CHUNKS)

    def forward(k):
        @pl.when(c >= 2)
        def _():
            chain_copy(k).wait_recv()

            @pl.when(c + 2 < C)
            def _():
                chain_copy(k).start()
            sib_copy(k).start()

    for k in range(ANY_EARLY):
        forward(k)
    forward(CHUNKS)
    forward(CHUNKS + 1)

    own = pl.ds(pl.multiple_of(r * ch, ch), ch)
    total = pm[own, :]
    for off in range(1, R):
        rs_copy(off).wait_recv()
        total = total + rsbuf[off - 1]
    pf[own, :] = total
    for off in range(1, R):
        ag_copy(off).start()

    left = list(range(ANY_EARLY, CHUNKS))

    def some(count):
        for _ in range(min(count, len(left))):
            forward(left.pop(0))

    sib_in(CHUNKS).wait_recv()
    sib_in(CHUNKS + 1).wait_recv()
    upper00 = jnp.where(sub <= lane, exact(linv_ref[0], dh[0, 0:nb, :]), 0.0)
    res[0] = upper_inverse(upper00, sub, lane)
    some(1)
    res[1] = exact(dh[0, nb:two, :], res[0])
    upper01 = exact(linv_ref[0], dh[1, 0:nb, :])
    rest = dh[1, nb:two, :] - exact(res[1], upper01)
    upper11 = jnp.where(sub <= lane, exact(linv_ref[1], rest), 0.0)
    res[2] = -exact(res[0], upper01)
    some(1)
    res[3] = upper_inverse(upper11, sub, lane)
    some(2)
    res[2] = exact(res[2], res[3])
    mixed = -exact(exact(linv_ref[1], res[1]), linv_ref[0])
    some(1)

    for q in range(2):
        @pl.when(r != q)
        def _():
            part = tops.at[q * nb:(q + 1) * nb]
            remote(part, part, to_s.at[0], to_r.at[q], row_peer(1)).wait_recv()

    for t in range(width // nb):
        spots = slice(t * nb, (t + 1) * nb)
        placed = select(sel[...], tops[:, spots])
        asw[:, spots] = jnp.where(hit[...] > 0.5, placed, a_v[:, spots])
        some(1)

    for off in range(1, R):
        ag_in(off).wait_recv()

    inv_low0 = linv_ref[0]
    inv_low1 = linv_ref[1]
    u_f[0:nb, :] = dot3(halves(inv_low0), halves(pf[0:nb, :]))
    u_f[nb:two, :] = (dot3(halves(mixed), halves(pf[0:nb, :]))
                      + dot3(halves(inv_low1), halves(pf[nb:two, :])))
    high, low = halves(u_f[...])
    u_hi[...] = high
    u_lo[...] = low

    step = height // TILES
    inv0 = halves(res[0])
    cross = halves(res[2])
    inv1 = halves(res[3])

    def update(t, start):
        spots = pl.ds(start, step)
        left0 = halves(pan[0, spots, :])
        left1 = halves(pan[1, spots, :])
        low0 = dot3(left0, inv0)
        low1 = dot3(left0, cross) + dot3(left1, inv1)
        high, low = halves(jnp.concatenate([low0, low1], axis=1))
        asw[spots, :] = asw[spots, :] - dot3((high, low), (u_hi[...], u_lo[...]))

        @pl.when(c == 0)
        def _():
            asw[spots, 0:nb] = low0

        @pl.when(c == 1)
        def _():
            asw[spots, 0:nb] = low1

    per_tile = CHUNKS // TILES
    for t in range(TILES):
        some(1)
        while left and left[0] < (t + 1) * per_tile:
            some(1)
        for k in range(t * per_tile, (t + 1) * per_tile):
            sib_in(k).wait_recv()
        update(t, t * step)
        if t == 0:
            @pl.when(r == 0)
            def _():
                asw[0:nb, :] = u_f[0:nb, :]

                @pl.when(c == 0)
                def _():
                    asw[0:nb, 0:nb] = jnp.where(sub <= lane, u_f[0:nb, 0:nb], 0.0)

            @pl.when(r == 1)
            def _():
                asw[0:nb, :] = u_f[nb:two, :]

                @pl.when(c == 0)
                def _():
                    asw[0:nb, 0:nb] = res[1]

                @pl.when(c == 1)
                def _():
                    asw[0:nb, 0:nb] = jnp.where(sub <= lane, u_f[nb:two, 0:nb], 0.0)

    for off in range(1, R):
        rs_copy(off).wait_send()
        ag_copy(off).wait_send()

    @pl.when(is_top)
    def _():
        for off in range(1, R):
            tops_copy(off).wait_send()

        @pl.when(at_root)
        def _():
            for off in range(1, R):
                tp_copy(off).wait_send()

    for k in range(CHUNKS + 2):
        sib_copy(k).wait_send()

        @pl.when(c + 2 < C)
        def _():
            chain_copy(k).wait_send()

    @pl.when(at_root)
    def _():
        for off in range(1, R):
            d_copy(off).wait_send()


def any_device(matrix, pivots, lower_inverse):
    R = lax.axis_size("row")
    C = lax.axis_size("col")
    height, width = matrix.shape
    nb = lower_inverse.shape[1]
    two = 2 * nb
    dma = pltpu.SemaphoreType.DMA
    vm = pltpu.VMEM
    return pl.pallas_call(
        functools.partial(any_kernel, R, C, nb),
        out_shape=jax.ShapeDtypeStruct((height, width), F32),
        in_specs=[pl.BlockSpec(memory_space=pl.ANY)] * 3,
        out_specs=pl.BlockSpec(memory_space=pltpu.VMEM),
        scratch_shapes=[
            vm((height, width), F32), vm((2, nb), jnp.int32), vm((2, nb, nb), F32),
            vm((height, two), BF16), vm((two, height), BF16),
            vm((two, width), F32), vm((two, width), F32),
            vm((R - 1, two // R, width), F32), vm((two, width), F32),
            vm((two, nb), F32), vm((two, nb), F32), vm((R - 1, two, nb), F32),
            vm((2, two, nb), F32), vm((2, height, nb), F32), vm((4, nb, nb), F32),
            vm((two, width), BF16), vm((two, width), BF16), vm((two, width), F32),
            vm((height, nb), F32),
            dma, dma, dma, dma((R - 1,)), dma((R - 1,)), dma((R - 1,)), dma((2,)),
            dma((R - 1,)), dma((R - 1,)), dma((R - 1,)), dma((R - 1,)),
            dma((R - 1,)), dma((2,)), dma((CHUNKS + 2,)), dma((CHUNKS + 2,)),
            dma((CHUNKS + 2,)), dma((CHUNKS + 2,)),
        ],
        compiler_params=pltpu.CompilerParams(
            collective_id=1, has_side_effects=True, vmem_limit_bytes=50 * 1024 * 1024),
    )(matrix, pivots, lower_inverse)


def most_kernel(R, nb, piv_ref, out_ref):
    owner = jnp.bitwise_and(jnp.right_shift(piv_ref[...], nb.bit_length() - 1), R - 1)
    most = jnp.zeros((2, 1), F32)
    for q in range(R):
        most = jnp.maximum(most, jnp.sum(jnp.where(owner == q, 1.0, 0.0), axis=1, keepdims=True))
    out_ref[0] = jnp.max(most).astype(jnp.int32)


def on_device(matrix, pivots, lower_inverse):
    R = lax.axis_size("row")
    nb = lower_inverse.shape[1]
    most = pl.pallas_call(
        functools.partial(most_kernel, R, nb),
        out_shape=jax.ShapeDtypeStruct((1,), jnp.int32),
        in_specs=[pl.BlockSpec(memory_space=pltpu.VMEM)],
        out_specs=pl.BlockSpec(memory_space=pltpu.SMEM),
    )(pivots)
    return lax.cond(most[0] <= room(R, nb), even_device, any_device, matrix, pivots, lower_inverse)


def solution(mesh):
    return jax.shard_map(
        on_device,
        mesh=mesh,
        in_specs=(P("row", "col"), P(), P()),
        out_specs=P("row", "col"),
        check_vma=False,
    )
```

```python
import functools

import jax
import jax.numpy as jnp
from jax import lax
from jax.experimental import pallas as pl
from jax.experimental.pallas import tpu as pltpu
from jax.sharding import PartitionSpec as P

MESH = pl.DeviceIdType.MESH
F32 = jnp.float32
BF16 = jnp.bfloat16
CHUNKS = 16
EARLY = 0
MIDDLE = 12
ANY_EARLY = 3
FAR = 4
INNER = (1, 2, 2, 2)
LAST = (1, 1, 0, 2)
PASS = 0
LATE_TILE = 3
BRING = 1
TILES = 4


def mm(left, right):
    return jnp.dot(left, right, preferred_element_type=F32)


def exact(left, right):
    return jnp.dot(left, right, precision=lax.Precision.HIGHEST, preferred_element_type=F32)


def halves(value):
    high = value.astype(BF16)
    return high, (value - high.astype(F32)).astype(BF16)


def thirds(value):
    high = value.astype(BF16)
    rest = value - high.astype(F32)
    middle = rest.astype(BF16)
    return high, middle, (rest - middle.astype(F32)).astype(BF16)


def select(chosen, value):
    high, middle, low = thirds(value)
    return mm(chosen, high) + (mm(chosen, middle) + mm(chosen, low))


def dot3(left, right):
    left_high, left_low = left
    right_high, right_low = right
    return mm(left_high, right_high) + (mm(left_low, right_high) + mm(left_high, right_low))


def upper_inverse(upper, rows, cols):
    on_diag = rows == cols
    eye = jnp.where(on_diag, 1.0, 0.0)
    kept = jnp.where(on_diag, upper, 0.0)
    scaled = upper / jnp.sum(kept, axis=1, keepdims=True)
    power = jnp.where(rows < cols, -scaled, 0.0)
    result = eye + power
    reach = 2
    while reach < upper.shape[0]:
        power = exact(power, power)
        result = result + exact(result, power)
        reach = reach * 2
    return result / jnp.sum(kept, axis=0, keepdims=True)


def select2(chosen, value):
    high, low = halves(value)
    return mm(chosen, high) + mm(chosen, low)


def close(left, right):
    left_high, left_low = halves(left)
    right_high, right_low = halves(right)
    return mm(jnp.concatenate([left_high, left_low, left_high], axis=1),
              jnp.concatenate([right_high, right_high, right_low], axis=0))


def quick_inverse(upper, rows, cols, between):
    on_diag = rows == cols
    eye = jnp.where(on_diag, 1.0, 0.0)
    kept = jnp.where(on_diag, upper, 0.0)
    scaled = upper / jnp.sum(kept, axis=1, keepdims=True)
    power = jnp.where(rows < cols, -scaled, 0.0)
    result = eye + power
    reach = 2
    while reach < upper.shape[0]:
        power = close(power, power)
        result = result + close(result, power)
        reach = reach * 2
        if reach in (8, 32):
            between(1)
    return result / jnp.sum(kept, axis=0, keepdims=True)


def room(R, nb):
    return (nb // R + 31) // 16 * 16


def kernel(R, C, nb, a_hbm, piv_ref, linv_ref, asw,
           sel, sel_t, place, split, tcomp, pall, dall, tops, tpan, dh, pan, res, inv3, me3, w3, tw, u_f, hit,
           load_sem, tq_s, tq_r, da_s, da_r, to_s, to_r,
           ag_s, ag_r, ch_s, ch_r, sb_s, sb_r):
    height, width = asw.shape
    two = 2 * nb
    cap = room(R, nb)
    W = 2 * cap
    ck = height // CHUNKS
    NJ = width // nb
    r = lax.axis_index("row")
    c = lax.axis_index("col")
    s = lax.rem(c, 2)
    sibling = {"col": c + 1 - 2 * s}
    top_half = jnp.minimum(r, 1)
    odd = lax.rem(r, 2)
    relay = R == 4

    def flip(bit):
        if bit == 1:
            return r + 1 - 2 * odd
        if bit == 2:
            return lax.rem(r + 2, 4)
        return 3 - r

    def cols(j):
        return pl.ds(j * nb, nb)

    def load(j):
        return pltpu.make_async_copy(a_hbm.at[:, cols(j)], asw.at[:, cols(j)], load_sem.at[j])

    for j in range(NJ):
        load(j).start()

    has_after = c + 2 < C
    has_before = c >= 2
    at_root = c < 2
    is_top = r < 2

    barrier = pltpu.get_barrier_semaphore()
    for off in range(1, R):
        pl.semaphore_signal(barrier, inc=1, device_id={"row": lax.rem(r + off, R)}, device_id_type=MESH)

    @pl.when(has_after)
    def _():
        pl.semaphore_signal(barrier, inc=1, device_id={"col": jnp.minimum(c + 2, C - 1)}, device_id_type=MESH)

    @pl.when(has_before)
    def _():
        pl.semaphore_signal(barrier, inc=1, device_id={"col": jnp.maximum(c - 2, 0)}, device_id_type=MESH)

    pl.semaphore_signal(barrier, inc=1, device_id=sibling, device_id_type=MESH)

    pl.semaphore_wait(barrier, R + jnp.minimum(c // 2, 1) + jnp.minimum((C - 1 - c) // 2, 1))

    def remote(src, dst, send, recv, where):
        return pltpu.make_async_remote_copy(
            src_ref=src, dst_ref=dst, send_sem=send, recv_sem=recv, device_id=where, device_id_type=MESH)

    def rows(index, count):
        return pl.ds(pl.multiple_of(index * count, count), count)

    def peer(off):
        return lax.rem(r + off, R)

    def origin(off):
        return lax.rem(r - off + R, R)

    def da_copy(off):
        part = dall.at[s, rows(r, W)]
        return remote(part, part, da_s.at[off - 1], da_r.at[off - 1], {"row": peer(off)})

    def da_in(off):
        part = dall.at[s, rows(origin(off), W)]
        return remote(part, part, da_s.at[off - 1], da_r.at[off - 1], {"row": peer(off)})

    def tq_copy(off):
        return remote(tcomp.at[0, rows(peer(off), cap)], tpan.at[s, rows(top_half, cap)],
                      tq_s.at[off - 1], tq_r.at[top_half], {"row": peer(off)})

    def tz_copy(off):
        return remote(tcomp.at[0, rows(peer(off), cap)], tops.at[0, rows(top_half, cap)],
                      tq_s.at[off - 1], tq_r.at[top_half], {"row": peer(off)})

    def to_copy(off):
        return remote(tcomp.at[pl.ds(1, NJ - 1), rows(peer(off), cap)],
                      tops.at[pl.ds(1, NJ - 1), rows(top_half, cap)],
                      to_s.at[off - 1], to_r.at[top_half], {"row": peer(off)})

    def tq_in(half):
        part = tpan.at[s, pl.ds(half * cap, cap)]
        return remote(part, part, tq_s.at[0], tq_r.at[half], {"row": peer(1)})

    def tz_in(half):
        part = tops.at[0, pl.ds(half * cap, cap)]
        return remote(part, part, tq_s.at[0], tq_r.at[half], {"row": peer(1)})

    def to_in(half):
        part = tops.at[pl.ds(1, NJ - 1), pl.ds(half * cap, cap)]
        return remote(part, part, to_s.at[0], to_r.at[half], {"row": peer(1)})

    def from_tops(copy):
        for half in range(2):
            @pl.when(r != half)
            def _():
                copy(half).wait_recv()

    def ag_copy(j, i):
        at = j * (R - 1) + i
        if not relay:
            part = pall.at[j, rows(r, W)]
            return remote(part, part, ag_s.at[at], ag_r.at[at], {"row": peer(i + 1)})
        if i < 2:
            part = pall.at[j, rows(r, W)]
            return remote(part, part, ag_s.at[at], ag_r.at[at], {"row": flip(i + 1)})
        bit = 1 + j % 2
        part = pall.at[j, rows(flip(3 - bit), W)]
        return remote(part, part, ag_s.at[at], ag_r.at[at], {"row": flip(bit)})

    def ag_in(j, i):
        at = j * (R - 1) + i
        src = flip(i + 1) if relay else origin(i + 1)
        part = pall.at[j, rows(src, W)]
        return remote(part, part, ag_s.at[at], ag_r.at[at], {"row": peer(1)})

    def ag_start(j):
        for i in range(2 if relay else R - 1):
            ag_copy(j, i).start()

    def ag_relay_from(j):
        return 1 - j % 2

    def past_root(j, go):
        if j == 0:
            pl.when(has_before)(go)
        else:
            go()

    def ag_pass(j):
        if relay:
            def go():
                ag_in(j, ag_relay_from(j)).wait_recv()
                ag_copy(j, 2).start()
            past_root(j, go)

    def ag_finish(j):
        def go():
            for i in range(R - 1):
                if not (relay and i == ag_relay_from(j)):
                    ag_in(j, i).wait_recv()
        past_root(j, go)

    TQ, DQ = CHUNKS, CHUNKS + 1

    def piece(k):
        if k < CHUNKS:
            return pan.at[s, pl.ds(k * ck, ck)]
        if k == TQ:
            return tpan.at[s, pl.ds(0, W)]
        return dall.at[s, rows(r, W)]

    after = {"col": jnp.minimum(c + 2, C - 2 + s)}

    def chain_copy(k):
        return remote(piece(k), piece(k), ch_s.at[k], ch_r.at[k], after)

    def root_copy(k):
        return remote(a_hbm.at[pl.ds(k * ck, ck), cols(0)], piece(k), ch_s.at[k], ch_r.at[k], after)

    step = height // TILES
    tiles = [(t * step, step) for t in range(TILES - 1)]
    tiles += [(height - step, step // 2), (height - step // 2, step // 2)]
    closing = {(start + count) // ck - 1: at for at, (start, count) in enumerate(tiles)}

    def spread(k, side):
        if k < CHUNKS:
            return pan.at[side, pl.ds(*tiles[k])]
        return tpan.at[side, pl.ds(0, W)] if k == TQ else dall.at[side]

    def sib_copy(k):
        return remote(spread(k, s), spread(k, s), sb_s.at[k], sb_r.at[k], sibling)

    def root_sib(k):
        return remote(a_hbm.at[pl.ds(*tiles[k]), cols(0)], spread(k, s), sb_s.at[k], sb_r.at[k], sibling)

    def sib_in(k):
        return remote(spread(k, 1 - s), spread(k, 1 - s), sb_s.at[k], sb_r.at[k], sibling)

    def forward(k, inner):
        @pl.when(has_before & (has_after if inner else c + 2 >= C))
        def _():
            chain_copy(k).wait_recv()
            if inner:
                chain_copy(k).start()
            if k == DQ:
                for off in range(1, R):
                    da_copy(off).start()
            elif k == TQ:
                sib_copy(TQ).start()
            elif k in closing:
                sib_copy(closing[k]).start()

    order = list(range(EARLY)) + [DQ] + list(range(EARLY, MIDDLE)) + [TQ] + list(range(MIDDLE, CHUNKS))
    left = order[:]
    late = order[:]

    def step_on(queue, count):
        for _ in range(min(count, len(queue))):
            forward(queue.pop(0), queue is left)

    def some(count):
        step_on(left, count)
        step_on(late, count)

    def until(k):
        for queue in (left, late):
            while k in queue:
                step_on(queue, 1)

    def from_root(first, last):
        for k in range(first, last):
            @pl.when(has_after)
            def _():
                root_copy(k).start()
            if k in closing:
                root_sib(closing[k]).start()

    @pl.when(at_root)
    def _():
        from_root(0, EARLY)

    shift = nb.bit_length() - 1
    rshift = R.bit_length() - 1
    lane = lax.broadcasted_iota(jnp.int32, (nb, nb), 1)
    sub = lax.broadcasted_iota(jnp.int32, (nb, nb), 0)
    lane_f = lane.astype(F32)
    sub_f = sub.astype(F32)
    before = jnp.where(sub < lane, 1.0, 0.0).astype(BF16)
    owners, slots, talls = [], [], []
    for k in range(2):
        p = piv_ref[k:k + 1, :]
        block = jnp.right_shift(p, shift)
        owner = jnp.bitwise_and(block, R - 1)
        local = jnp.left_shift(jnp.right_shift(block, rshift), shift) + jnp.bitwise_and(p, nb - 1)
        hot = jnp.where(jnp.broadcast_to(owner, (16, nb)) == sub[0:16], 1.0, 0.0)
        rank = mm(hot.astype(BF16), before)
        slot = jnp.sum(hot * rank, axis=0, keepdims=True)
        mine = jnp.where(owner == r, slot, -1.0)
        match = jnp.broadcast_to(mine, (cap, nb)) == sub_f[0:cap]
        value = jnp.broadcast_to(local.astype(F32) + 1.0, (cap, nb))
        spot = jnp.sum(jnp.where(match, value, 0.0), axis=1, keepdims=True) - 1.0
        owners.append(owner)
        slots.append(slot)
        talls.append(jnp.broadcast_to(spot, (cap, nb)))
    if W < nb:
        talls.append(jnp.full((nb - W, nb), -1.0, F32))
    tall = jnp.concatenate(talls, axis=0)
    for t in range(height // nb):
        spots = slice(t * nb, (t + 1) * nb)
        sel_t[:, spots] = jnp.where(tall[0:W] == lane_f[0:W] + float(t * nb), 1.0, 0.0).astype(BF16)

    load(0).wait()
    first = select(sel_t[...], asw[:, 0:nb])

    @pl.when(at_root)
    def _():
        dall[s, rows(r, W), :] = first

        @pl.when(has_after)
        def _():
            chain_copy(DQ).start()
        for off in range(1, R):
            da_copy(off).start()
        from_root(EARLY, MIDDLE)
        pan[s] = asw[:, 0:nb]

    @pl.when(has_before)
    def _():
        pall[0, rows(r, W), :] = first
        ag_start(0)

    def collect(start, stop):
        value = select2(sel_t[...], asw[:, start * nb:stop * nb])
        for j in range(start, stop):
            pall[j, rows(r, W), :] = value[:, (j - start) * nb:(j - start + 1) * nb]

    load(1).wait()
    collect(1, 2)
    for j in range(2, NJ):
        load(j).wait()
    for j in range(2, NJ, 2):
        collect(j, min(j + 2, NJ))

    @pl.when(c >= FAR)
    def _():
        for j in range(1, NJ):
            ag_start(j)

    if W < nb:
        for j in range(NJ):
            tops[j, W:nb, :] = jnp.zeros((nb - W, nb), F32)
        for k in range(2):
            tpan[k, W:nb, :] = jnp.zeros((nb - W, nb), F32)
    wide = tall.T
    for t in range(height // nb):
        spots = slice(t * nb, (t + 1) * nb)
        value = jnp.where(wide == sub_f + float(t * nb), 1.0, 0.0).astype(BF16)
        sel[spots, 0:nb] = value
        sel[spots, nb:two] = value
    for k in range(2):
        aim = owners[k].astype(F32) * float(W) + (slots[k] + float(k * cap))
        aim = jnp.broadcast_to(aim, (nb, nb)).T
        for t in range(R * W // nb):
            place[k * nb:(k + 1) * nb, t * nb:(t + 1) * nb] = jnp.where(
                aim == lane_f + float(t * nb), 1.0, 0.0).astype(BF16)

    until(DQ)

    @pl.when(c < FAR)
    def _():
        for j in range(1, NJ):
            ag_start(j)

    @pl.when(is_top)
    def _():
        owner = jnp.where(r == 0, owners[0], owners[1])
        slot = jnp.where(r == 0, slots[0], slots[1])
        for q in range(R):
            aim = jnp.where(owner == q, slot, -1.0)
            aim = jnp.where(jnp.broadcast_to(aim, (cap, nb)) == sub_f[0:cap], 1.0, 0.0).astype(BF16)
            split[q * cap:(q + 1) * cap, 0:nb] = aim
            split[q * cap:(q + 1) * cap, nb:two] = aim
        value = mm(split[...], jnp.concatenate(halves(asw[0:nb, :]), axis=0))
        for j in range(NJ):
            tcomp[j] = value[:, j * nb:(j + 1) * nb]
        own = jnp.where(r == 0, value[0:cap, :], value[cap:2 * cap, :])

        @pl.when(at_root)
        def _():
            tpan[s, rows(top_half, cap), :] = own[:, 0:nb]
            for off in range(1, R):
                tq_copy(off).start()

        @pl.when(has_before)
        def _():
            tops[0, rows(top_half, cap), :] = own[:, 0:nb]
            for off in range(1, R):
                tz_copy(off).start()

        for off in range(1, R):
            to_copy(off).start()
        for j in range(1, NJ):
            tops[j, rows(top_half, cap), :] = own[:, j * nb:(j + 1) * nb]

    step_on(left, INNER[0])
    step_on(late, LAST[0])
    ones = jnp.full((two, nb), 1.0, BF16)

    @pl.loop(0, TILES)
    def _(t):
        spots = rows(t, height // TILES)
        hit[spots, :] = mm(sel[spots, :], ones)

    step_on(left, INNER[1])
    step_on(late, LAST[1])
    ag_pass(0)
    step_on(left, INNER[2])
    step_on(late, LAST[2])
    for off in range(1, R):
        da_in(off).wait_recv()
    sib_copy(DQ).start()

    step_on(left, INNER[3])
    step_on(late, LAST[3])
    sib_in(DQ).wait_recv()
    both = select(place[...], jnp.concatenate([dall[0], dall[1]], axis=1))
    dh[0] = both[:, 0:nb]
    dh[1] = both[:, nb:two]
    upper00 = jnp.where(sub <= lane, close(linv_ref[0], dh[0, 0:nb, :]), 0.0)
    upper01 = close(linv_ref[0], dh[1, 0:nb, :])
    some(1)
    ag_pass(1)
    ag_pass(2)
    res[0] = quick_inverse(upper00, sub, lane, some)
    some(1)
    ag_pass(3)
    @pl.when(at_root)
    def _():
        from_tops(tq_in)

        @pl.when(has_after)
        def _():
            chain_copy(TQ).start()
        sib_copy(TQ).start()
        from_root(MIDDLE, CHUNKS)
        tops[0] = tpan[s]
        pall[0] = dall[s]

    res[1] = close(dh[0, nb:two, :], res[0])
    rest = dh[1, nb:two, :] - close(res[1], upper01)
    upper11 = jnp.where(sub <= lane, close(linv_ref[1], rest), 0.0)
    res[2] = -close(res[0], upper01)
    mixed = -close(close(linv_ref[1], res[1]), linv_ref[0])
    blank = jnp.zeros((nb, nb), F32)
    high, low = halves(jnp.concatenate([
        jnp.concatenate([linv_ref[0], blank], axis=1),
        jnp.concatenate([mixed, linv_ref[1]], axis=1)], axis=0))
    span = R * W
    high = mm(high, place[...]).astype(BF16)
    me3[:, 0:span] = high
    me3[:, span:2 * span] = mm(low, place[...]).astype(BF16)
    me3[:, 2 * span:3 * span] = high
    some(1)
    res[3] = quick_inverse(upper11, sub, lane, some)
    for j in range(4 if PASS == 0 else 3, NJ):
        ag_pass(j)
    some(1)

    def stack(value):
        high, low = halves(value)
        return jnp.concatenate([high, high, low], axis=0)

    def row_stack(value):
        high, low = halves(value)
        return jnp.concatenate([high, low, high], axis=1)

    inverse = jnp.concatenate([
        jnp.concatenate([res[0], close(res[2], res[3])], axis=1),
        jnp.concatenate([blank, res[3]], axis=1)], axis=0)
    inv3[...] = stack(inverse)
    left3 = row_stack(inverse)
    for j in range(0, NJ, 2):
        ag_finish(j)
        ag_finish(j + 1)
        spots = slice(j * nb, (j + 2) * nb)
        value = mm(me3[...], stack(jnp.concatenate([pall[j], pall[j + 1]], axis=1)))
        u_f[:, spots] = value
        w3[:, spots] = stack(mm(left3, stack(value)))
        some(1)

    def update(start, count):
        spots = slice(start, start + count)
        here = hit[spots, :] > 0.5
        kept = row_stack(jnp.concatenate([
            jnp.where(here, 0.0, pan[0, spots, :]), jnp.where(here, 0.0, pan[1, spots, :])], axis=1))
        asw[spots, :] = asw[spots, :] - mm(kept, w3[...])

        @pl.when(at_root)
        def _():
            value = mm(kept, inv3[...])
            value = jnp.where(c == 0, value[:, 0:nb], value[:, nb:two])
            asw[spots, 0:nb] = jnp.where(here, asw[spots, 0:nb], value)

    def bring():
        until(TQ)
        sib_in(TQ).wait_recv()
        from_tops(to_in)

        @pl.when(has_before)
        def _():
            from_tops(tz_in)

        tp = row_stack(jnp.concatenate([tpan[0], tpan[1]], axis=1))
        moved = jnp.concatenate([tops[j] for j in range(NJ)], axis=1) - mm(tp, w3[...])
        tw[0:nb, :], tw[nb:two, :] = halves(moved)

        @pl.when(at_root)
        def _():
            value = mm(tp, inv3[...])
            tw[0:nb, 0:nb], tw[nb:two, 0:nb] = halves(jnp.where(c == 0, value[:, 0:nb], value[:, nb:two]))

        for t in range(TILES):
            spots = slice(t * step, (t + 1) * step)
            here = hit[spots, :] > 0.5
            moved = mm(sel[spots, :], tw[...])
            for j in range(NJ):
                part = slice(j * nb, (j + 1) * nb)
                asw[spots, part] = jnp.where(here, moved[:, part], asw[spots, part])
            some(BRING)

    def finish_top():
        @pl.when(r == 0)
        def _():
            asw[0:nb, :] = u_f[0:nb, :]

            @pl.when(c == 0)
            def _():
                asw[0:nb, 0:nb] = jnp.where(sub <= lane, u_f[0:nb, 0:nb], 0.0)

        @pl.when(r == 1)
        def _():
            asw[0:nb, :] = u_f[nb:two, :]

            @pl.when(c == 0)
            def _():
                asw[0:nb, 0:nb] = res[1]

            @pl.when(c == 1)
            def _():
                asw[0:nb, 0:nb] = jnp.where(sub <= lane, u_f[nb:two, 0:nb], 0.0)

    for at, (start, count) in enumerate(tiles):
        if at == LATE_TILE:
            bring()
            finish_top()
        for queue in (left, late):
            while any(k < CHUNKS and k * ck < start + count for k in queue):
                step_on(queue, 1)
        sib_in(at).wait_recv()
        update(start, count)
        some(1)

    for j in range(NJ):
        def gone(j=j):
            for i in range(R - 1):
                ag_copy(j, i).wait_send()
        past_root(j, gone)

    @pl.when(is_top)
    def _():
        for off in range(1, R):
            to_copy(off).wait_send()
            tq_copy(off).wait_send()

    for off in range(1, R):
        da_copy(off).wait_send()

    for k in list(range(len(tiles))) + [TQ, DQ]:
        sib_copy(k).wait_send()

    for k in range(CHUNKS + 2):
        @pl.when(has_after)
        def _():
            chain_copy(k).wait_send()


def even_device(matrix, pivots, lower_inverse):
    R = lax.axis_size("row")
    C = lax.axis_size("col")
    height, width = matrix.shape
    nb = lower_inverse.shape[1]
    two = 2 * nb
    nj = width // nb
    cap = room(R, nb)
    dma = pltpu.SemaphoreType.DMA
    vm = pltpu.VMEM
    return pl.pallas_call(
        functools.partial(kernel, R, C, nb),
        out_shape=jax.ShapeDtypeStruct((height, width), F32),
        in_specs=[pl.BlockSpec(memory_space=pl.ANY)] + [pl.BlockSpec(memory_space=pltpu.VMEM)] * 2,
        out_specs=pl.BlockSpec(memory_space=pltpu.VMEM),
        scratch_shapes=[
            vm((height, two), BF16), vm((2 * cap, height), BF16), vm((two, 2 * cap * R), BF16),
            vm((cap * R, two), BF16), vm((nj, cap * R, nb), F32), vm((nj, 2 * cap * R, nb), F32),
            vm((2, 2 * cap * R, nb), F32), vm((nj, nb, nb), F32), vm((2, nb, nb), F32),
            vm((2, two, nb), F32), vm((2, height, nb), F32), vm((4, nb, nb), F32),
            vm((3 * two, two), BF16), vm((two, 6 * cap * R), BF16),
            vm((3 * two, width), BF16), vm((two, width), BF16), vm((two, width), F32),
            vm((height, nb), F32),
            dma((nj,)), dma((R - 1,)), dma((2,)), dma((R - 1,)), dma((R - 1,)),
            dma((R - 1,)), dma((2,)),
            dma((nj * (R - 1),)), dma((nj * (R - 1),)),
            dma((CHUNKS + 2,)), dma((CHUNKS + 2,)), dma((CHUNKS + 2,)), dma((CHUNKS + 2,)),
        ],
        compiler_params=pltpu.CompilerParams(
            collective_id=0, has_side_effects=True, vmem_limit_bytes=50 * 1024 * 1024),
    )(matrix, pivots, lower_inverse)


def any_kernel(R, C, nb, a_hbm, piv_hbm, linv_hbm, asw,
           a_v, piv_ref, linv_ref, sel, sel_t, pm, pf, rsbuf, tops, tp, dpart, dbuf, dh, pan, res,
           u_hi, u_lo, u_f, hit,
           load_sem, piv_sem, linv_sem, d_s, d_r, tp_s, tp_r, rs_s, rs_r, ag_s, ag_r,
           to_s, to_r, ch_s, ch_r, sb_s, sb_r):
    height, width = a_v.shape
    two = 2 * nb
    ch = two // R
    ck = height // CHUNKS
    r = lax.axis_index("row")
    c = lax.axis_index("col")
    s = lax.rem(c, 2)
    sibling = {"col": c + 1 - 2 * s}

    load = pltpu.make_async_copy(a_hbm, a_v, load_sem)
    load_piv = pltpu.make_async_copy(piv_hbm, piv_ref, piv_sem)
    load_linv = pltpu.make_async_copy(linv_hbm, linv_ref, linv_sem)
    load_piv.start()
    load.start()
    load_linv.start()

    barrier = pltpu.get_barrier_semaphore()
    for off in range(1, R):
        pl.semaphore_signal(barrier, inc=1, device_id={"row": lax.rem(r + off, R)}, device_id_type=MESH)
    has_after = c + 2 < C
    has_before = c >= 2

    @pl.when(has_after)
    def _():
        pl.semaphore_signal(barrier, inc=1, device_id={"col": jnp.minimum(c + 2, C - 1)}, device_id_type=MESH)

    @pl.when(has_before)
    def _():
        pl.semaphore_signal(barrier, inc=1, device_id={"col": jnp.maximum(c - 2, 0)}, device_id_type=MESH)

    pl.semaphore_signal(barrier, inc=1, device_id=sibling, device_id_type=MESH)

    load_piv.wait()
    shift = nb.bit_length() - 1
    rshift = R.bit_length() - 1
    lane = lax.broadcasted_iota(jnp.int32, (nb, nb), 1)
    sub = lax.broadcasted_iota(jnp.int32, (nb, nb), 0)
    for k in range(2):
        p = piv_ref[k:k + 1, :]
        block = jnp.right_shift(p, shift)
        local = jnp.left_shift(jnp.right_shift(block, rshift), shift) + jnp.bitwise_and(p, nb - 1)
        local = jnp.where(jnp.bitwise_and(block, R - 1) == r, local, -1)
        wide = jnp.broadcast_to(local, (nb, nb))
        tall = wide.astype(F32).T
        for t in range(height // nb):
            spots = slice(t * nb, (t + 1) * nb)
            sel[spots, k * nb:(k + 1) * nb] = jnp.where(wide == sub + t * nb, 1.0, 0.0).astype(BF16)
            sel_t[k * nb:(k + 1) * nb, spots] = jnp.where(
                tall == (lane + t * nb).astype(F32), 1.0, 0.0).astype(BF16)

    load.wait()
    load_linv.wait()
    pl.semaphore_wait(barrier, R + jnp.minimum(c // 2, 1) + jnp.minimum((C - 1 - c) // 2, 1))

    def remote(src, dst, send, recv, where):
        return pltpu.make_async_remote_copy(
            src_ref=src, dst_ref=dst, send_sem=send, recv_sem=recv, device_id=where, device_id_type=MESH)

    def row_peer(off):
        return {"row": lax.rem(r + off, R)}

    def tp_copy(off):
        q = jnp.minimum(r, 1)
        return remote(a_v.at[0:nb, 0:nb], tp.at[pl.ds(pl.multiple_of(q * nb, nb), nb)],
                      tp_s.at[off - 1], tp_r.at[q], row_peer(off))

    def tops_copy(off):
        q = jnp.minimum(r, 1)
        return remote(a_v.at[0:nb], tops.at[pl.ds(pl.multiple_of(q * nb, nb), nb)],
                      to_s.at[off - 1], to_r.at[q], row_peer(off))

    def d_copy(off):
        return remote(dpart, dbuf.at[off - 1], d_s.at[off - 1], d_r.at[off - 1], row_peer(off))

    def rs_copy(off):
        to = lax.rem(r + off, R)
        return remote(pm.at[pl.ds(pl.multiple_of(to * ch, ch), ch)], rsbuf.at[off - 1],
                      rs_s.at[off - 1], rs_r.at[off - 1], {"row": to})

    def ag_copy(off):
        mine = pf.at[pl.ds(pl.multiple_of(r * ch, ch), ch)]
        return remote(mine, mine, ag_s.at[off - 1], ag_r.at[off - 1], row_peer(off))

    def ag_in(off):
        src = lax.rem(r - off + R, R)
        there = pf.at[pl.ds(pl.multiple_of(src * ch, ch), ch)]
        return remote(there, there, ag_s.at[off - 1], ag_r.at[off - 1], row_peer(off))

    def piece(side, k):
        if k < CHUNKS:
            return pan.at[side, pl.ds(k * ck, ck)]
        return dh.at[side, pl.ds((k - CHUNKS) * nb, nb)]

    def chain_copy(k):
        part = piece(s, k)
        return remote(part, part, ch_s.at[k], ch_r.at[k], {"col": jnp.minimum(c + 2, C - 2 + s)})

    def sib_copy(k):
        part = piece(s, k)
        return remote(part, part, sb_s.at[k], sb_r.at[k], sibling)

    def sib_in(k):
        part = piece(1 - s, k)
        return remote(part, part, sb_s.at[k], sb_r.at[k], sibling)

    is_top = r < 2
    at_root = c < 2

    @pl.when(at_root)
    def _():
        @pl.when(is_top)
        def _():
            for off in range(1, R):
                tp_copy(off).start()
            tp[pl.ds(pl.multiple_of(jnp.minimum(r, 1) * nb, nb), nb), :] = a_v[0:nb, 0:nb]

        dpart[...] = select(sel_t[...], a_v[:, 0:nb])
        for off in range(1, R):
            d_copy(off).start()

    ones = jnp.full((two, nb), 1.0, BF16)

    @pl.loop(0, TILES)
    def _(t):
        spots = pl.ds(pl.multiple_of(t * (height // TILES), height // TILES), height // TILES)
        hit[spots, :] = mm(sel[spots, :], ones)

    def panel(first, last):
        high, middle, low = thirds(tp[...])
        for k in range(first, last):
            spots = slice(k * ck, (k + 1) * ck)
            chosen = sel[spots, :]
            placed = mm(chosen, high) + (mm(chosen, middle) + mm(chosen, low))
            pan[s, spots, :] = jnp.where(hit[spots, :] > 0.5, placed, a_v[spots, 0:nb])
            chain_copy(k).start()
            sib_copy(k).start()

    @pl.loop(0, width // nb)
    def _(t):
        spots = pl.ds(pl.multiple_of(t * nb, nb), nb)
        pm[:, spots] = select(sel_t[...], a_v[:, spots])

    @pl.when(at_root)
    def _():
        for q in range(2):
            @pl.when(r != q)
            def _():
                part = tp.at[q * nb:(q + 1) * nb]
                remote(part, part, tp_s.at[0], tp_r.at[q], row_peer(1)).wait_recv()
        panel(0, ANY_EARLY)

    for off in range(1, R):
        rs_copy(off).start()

    @pl.when(is_top)
    def _():
        for off in range(1, R):
            tops_copy(off).start()
        tops[pl.ds(pl.multiple_of(jnp.minimum(r, 1) * nb, nb), nb), :] = a_v[0:nb, :]

    @pl.when(at_root)
    def _():
        total = dpart[...]
        for off in range(1, R):
            d_copy(off).wait_recv()
            total = total + dbuf[off - 1]
        dh[s] = total
        for k in range(CHUNKS, CHUNKS + 2):
            chain_copy(k).start()
            sib_copy(k).start()
        panel(ANY_EARLY, CHUNKS)

    def forward(k):
        @pl.when(c >= 2)
        def _():
            chain_copy(k).wait_recv()

            @pl.when(c + 2 < C)
            def _():
                chain_copy(k).start()
            sib_copy(k).start()

    for k in range(ANY_EARLY):
        forward(k)
    forward(CHUNKS)
    forward(CHUNKS + 1)

    own = pl.ds(pl.multiple_of(r * ch, ch), ch)
    total = pm[own, :]
    for off in range(1, R):
        rs_copy(off).wait_recv()
        total = total + rsbuf[off - 1]
    pf[own, :] = total
    for off in range(1, R):
        ag_copy(off).start()

    left = list(range(ANY_EARLY, CHUNKS))

    def some(count):
        for _ in range(min(count, len(left))):
            forward(left.pop(0))

    sib_in(CHUNKS).wait_recv()
    sib_in(CHUNKS + 1).wait_recv()
    upper00 = jnp.where(sub <= lane, exact(linv_ref[0], dh[0, 0:nb, :]), 0.0)
    res[0] = upper_inverse(upper00, sub, lane)
    some(1)
    res[1] = exact(dh[0, nb:two, :], res[0])
    upper01 = exact(linv_ref[0], dh[1, 0:nb, :])
    rest = dh[1, nb:two, :] - exact(res[1], upper01)
    upper11 = jnp.where(sub <= lane, exact(linv_ref[1], rest), 0.0)
    res[2] = -exact(res[0], upper01)
    some(1)
    res[3] = upper_inverse(upper11, sub, lane)
    some(2)
    res[2] = exact(res[2], res[3])
    mixed = -exact(exact(linv_ref[1], res[1]), linv_ref[0])
    some(1)

    for q in range(2):
        @pl.when(r != q)
        def _():
            part = tops.at[q * nb:(q + 1) * nb]
            remote(part, part, to_s.at[0], to_r.at[q], row_peer(1)).wait_recv()

    for t in range(width // nb):
        spots = slice(t * nb, (t + 1) * nb)
        placed = select(sel[...], tops[:, spots])
        asw[:, spots] = jnp.where(hit[...] > 0.5, placed, a_v[:, spots])
        some(1)

    for off in range(1, R):
        ag_in(off).wait_recv()

    inv_low0 = linv_ref[0]
    inv_low1 = linv_ref[1]
    u_f[0:nb, :] = dot3(halves(inv_low0), halves(pf[0:nb, :]))
    u_f[nb:two, :] = (dot3(halves(mixed), halves(pf[0:nb, :]))
                      + dot3(halves(inv_low1), halves(pf[nb:two, :])))
    high, low = halves(u_f[...])
    u_hi[...] = high
    u_lo[...] = low

    step = height // TILES
    inv0 = halves(res[0])
    cross = halves(res[2])
    inv1 = halves(res[3])

    def update(t, start):
        spots = pl.ds(start, step)
        left0 = halves(pan[0, spots, :])
        left1 = halves(pan[1, spots, :])
        low0 = dot3(left0, inv0)
        low1 = dot3(left0, cross) + dot3(left1, inv1)
        high, low = halves(jnp.concatenate([low0, low1], axis=1))
        asw[spots, :] = asw[spots, :] - dot3((high, low), (u_hi[...], u_lo[...]))

        @pl.when(c == 0)
        def _():
            asw[spots, 0:nb] = low0

        @pl.when(c == 1)
        def _():
            asw[spots, 0:nb] = low1

    per_tile = CHUNKS // TILES
    for t in range(TILES):
        some(1)
        while left and left[0] < (t + 1) * per_tile:
            some(1)
        for k in range(t * per_tile, (t + 1) * per_tile):
            sib_in(k).wait_recv()
        update(t, t * step)
        if t == 0:
            @pl.when(r == 0)
            def _():
                asw[0:nb, :] = u_f[0:nb, :]

                @pl.when(c == 0)
                def _():
                    asw[0:nb, 0:nb] = jnp.where(sub <= lane, u_f[0:nb, 0:nb], 0.0)

            @pl.when(r == 1)
            def _():
                asw[0:nb, :] = u_f[nb:two, :]

                @pl.when(c == 0)
                def _():
                    asw[0:nb, 0:nb] = res[1]

                @pl.when(c == 1)
                def _():
                    asw[0:nb, 0:nb] = jnp.where(sub <= lane, u_f[nb:two, 0:nb], 0.0)

    for off in range(1, R):
        rs_copy(off).wait_send()
        ag_copy(off).wait_send()

    @pl.when(is_top)
    def _():
        for off in range(1, R):
            tops_copy(off).wait_send()

        @pl.when(at_root)
        def _():
            for off in range(1, R):
                tp_copy(off).wait_send()

    for k in range(CHUNKS + 2):
        sib_copy(k).wait_send()

        @pl.when(c + 2 < C)
        def _():
            chain_copy(k).wait_send()

    @pl.when(at_root)
    def _():
        for off in range(1, R):
            d_copy(off).wait_send()


def any_device(matrix, pivots, lower_inverse):
    R = lax.axis_size("row")
    C = lax.axis_size("col")
    height, width = matrix.shape
    nb = lower_inverse.shape[1]
    two = 2 * nb
    dma = pltpu.SemaphoreType.DMA
    vm = pltpu.VMEM
    return pl.pallas_call(
        functools.partial(any_kernel, R, C, nb),
        out_shape=jax.ShapeDtypeStruct((height, width), F32),
        in_specs=[pl.BlockSpec(memory_space=pl.ANY)] * 3,
        out_specs=pl.BlockSpec(memory_space=pltpu.VMEM),
        scratch_shapes=[
            vm((height, width), F32), vm((2, nb), jnp.int32), vm((2, nb, nb), F32),
            vm((height, two), BF16), vm((two, height), BF16),
            vm((two, width), F32), vm((two, width), F32),
            vm((R - 1, two // R, width), F32), vm((two, width), F32),
            vm((two, nb), F32), vm((two, nb), F32), vm((R - 1, two, nb), F32),
            vm((2, two, nb), F32), vm((2, height, nb), F32), vm((4, nb, nb), F32),
            vm((two, width), BF16), vm((two, width), BF16), vm((two, width), F32),
            vm((height, nb), F32),
            dma, dma, dma, dma((R - 1,)), dma((R - 1,)), dma((R - 1,)), dma((2,)),
            dma((R - 1,)), dma((R - 1,)), dma((R - 1,)), dma((R - 1,)),
            dma((R - 1,)), dma((2,)), dma((CHUNKS + 2,)), dma((CHUNKS + 2,)),
            dma((CHUNKS + 2,)), dma((CHUNKS + 2,)),
        ],
        compiler_params=pltpu.CompilerParams(
            collective_id=1, has_side_effects=True, vmem_limit_bytes=50 * 1024 * 1024),
    )(matrix, pivots, lower_inverse)


def most_kernel(R, nb, piv_ref, out_ref):
    owner = jnp.bitwise_and(jnp.right_shift(piv_ref[...], nb.bit_length() - 1), R - 1)
    most = jnp.zeros((2, 1), F32)
    for q in range(R):
        most = jnp.maximum(most, jnp.sum(jnp.where(owner == q, 1.0, 0.0), axis=1, keepdims=True))
    out_ref[0] = jnp.max(most).astype(jnp.int32)


def on_device(matrix, pivots, lower_inverse):
    R = lax.axis_size("row")
    nb = lower_inverse.shape[1]
    most = pl.pallas_call(
        functools.partial(most_kernel, R, nb),
        out_shape=jax.ShapeDtypeStruct((1,), jnp.int32),
        in_specs=[pl.BlockSpec(memory_space=pltpu.VMEM)],
        out_specs=pl.BlockSpec(memory_space=pltpu.SMEM),
    )(pivots)
    return lax.cond(most[0] <= room(R, nb), even_device, any_device, matrix, pivots, lower_inverse)


def solution(mesh):
    return jax.shard_map(
        on_device,
        mesh=mesh,
        in_specs=(P("row", "col"), P(), P()),
        out_specs=P("row", "col"),
        check_vma=False,
    )
```
